256 devices in a mesh: cache: 64 (over y, z, core), tensor: 4 (over x).
Axes of the slice: x: 4, y: 4, z: 8, core: 2. Of those that a mesh axis runs over, the one named last changes fastest.
Arguments:
- hidden: bfloat16 [512, 4, 7168], P('cache', None, 'tensor'), may hold values from -6 to 6
- w_dkv: bfloat16 [7168, 576], P('tensor'), may hold values from -0.0625 to 0.0625
- kv_gain: float32 [512], replicated, may hold values from 0.5 to 1.5
- q_latent: bfloat16 [512, 4, 32768], P('cache', None, 'tensor'), may hold values from -6 to 6
- q_rope: bfloat16 [512, 4, 4096], P('cache', None, 'tensor'), may hold values from -6 to 6
- w_uv: bfloat16 [64, 512, 128], P('tensor'), may hold values from -0.25 to 0.25
- latent_cache: bfloat16 [4096, 64, 576], P('cache'), may hold values from -6 to 6
- block_slots: int32 [512, 64], P('cache'), may hold values from 0 to 63
- seg_owner: int32 [512, 8], P('cache'), may hold values from 0 to 63, all different within a row; in each aligned block of 8 rows (0 to 7, 8 to 15, ...) at most 2 rows name the same one
- lengths: int32 [512], P('cache'), may hold values from 1 to 4096
Outputs:
- attn_out: bfloat16 [512, 4, 8192], P('cache', None, 'tensor')
- new_latent: bfloat16 [512, 4, 576], P('cache')
The draws below stay inside these ranges and needn't reach their ends.
Inputs may be any that keep to these rules, and one draw needn't show every extreme that they name: `seg_owner`: in each row the 8 owners are distinct. Among the rows of one device no owner is named more than 2 times, a bound that some block reaches.
All inputs are finite; a program needn't handle non-finite values.
Results may differ from the reference program's by a relative error of at most 0.0053.
Values may be sent and summed in bfloat16 or wider, within the bound.
No kernel may reach another device: no remote copies, remote signals or barrier semaphores. Data moves between devices by JAX's collectives and lax.ppermute only.
A program may use at most 128 MiB of HBM per device.

```python
import math
import jax
import jax.numpy as jnp
import numpy as np
from jax import lax

D = 7168
HEADS = 64
LAT = 512
ROPE = 64
VH = 128
BT = 64
NB = 64
SEGS = 8
STEPS = 4
ROWS_DEV = 8
BLK_DEV = 64
ROWS = 512
BLOCKS = 4096
CAP = 2
N_CACHE = 64


def draw_latent_cache(key, part):
    key = jax.random.fold_in(key, 7)
    values = jnp.clip(jax.random.normal(key, (BLOCKS, BT, LAT + ROPE), jnp.float32), -6.0, 6.0)
    return values.astype(jnp.bfloat16)


def draw_q_latent(key, part):
    key = jax.random.fold_in(key, 13)
    key_values = jax.random.fold_in(key, 0)
    values = jnp.clip(jax.random.normal(key_values, (ROWS, STEPS, HEADS, LAT), jnp.float32), -6.0, 6.0)
    return values.reshape(ROWS, STEPS, HEADS * LAT).astype(jnp.bfloat16)


def with_ends(drawn, own_key, smallest, high):
    longest = drawn.shape.index(max(drawn.shape))
    spots = []
    for shift in (0, 1):
        where = [jax.random.randint(jax.random.fold_in(own_key, axis), (), 0, length) for axis, length in enumerate(drawn.shape)]
        where[longest] = (where[longest] + shift) % drawn.shape[longest]
        spots.append(tuple(where))
    return drawn.at[spots[0]].set(smallest).at[spots[1]].set(high)


def shard_levels(own_key, dims, cuts, least, high):
    def one(position, parts):
        draws = jax.random.uniform(jax.random.fold_in(jax.random.fold_in(own_key, 6), position), (parts,), jnp.float32, least / len(cuts), high / len(cuts))
        return jnp.repeat(jnp.exp(draws), dims[position] // parts).reshape((-1,) + (1,) * (len(dims) - position - 1))

    factor_of = one(*cuts[0])
    for cut in cuts[1:]:
        factor_of = factor_of * one(*cut)
    return factor_of


def rank_bounds(amount, skew):
    portions = [(1 << 20) // math.isqrt(grade ** skew) + 1 for grade in range(1, amount + 1)]
    width = 1 + sum(portions) // (1 << 30)
    return np.cumsum(np.array([max(1, weight // width) for weight in portions]))


def ranked(rng, extent, number_of, skew):
    grid = rank_bounds(number_of, skew)
    ticket = jax.random.randint(jax.random.fold_in(rng, 1), extent, 0, int(grid[number_of - 1]))
    grade = jnp.searchsorted(jnp.asarray(grid, jnp.int32), ticket, side="right")
    return jax.random.permutation(jax.random.fold_in(rng, 2), number_of)[grade].astype(jnp.int32)


def shared_out(stream_key, own, number, rows, number_of, top, limit, slope):
    order = jax.random.permutation(stream_key, number_of)
    crowded, usual = portions_of(number_of, rows * top, limit, slope, True), portions_of(number_of, rows * top, limit, slope, False)
    places = jnp.arange(number_of)

    def named(sizes, turn):
        used = int((sizes > 0).sum())
        fixed = max(1, used // 4)
        passed = fixed + (places - fixed + turn * (used - fixed)) % max(1, number_of - fixed)
        return jnp.zeros((number_of,), jnp.int32).at[order[jnp.where(places < fixed, places, passed)]].set(jnp.asarray(sizes, jnp.int32))

    sizes = jnp.where(number % 4 == 0, named(crowded, number // 4), named(usual, number - number // 4 - 1))
    mixed = jax.random.permutation(jax.random.fold_in(own, 3), number_of)
    giver, taker = mixed[0:number_of // 2 * 2:2], mixed[1:number_of // 2 * 2:2]
    margin = jnp.minimum(sizes[giver] - 1, limit - sizes[taker]) // 2
    margin = jnp.where((giver == order[0]) | (taker == order[0]) | (sizes[taker] == 0), 0, jnp.maximum(margin, 0))
    passed = jax.random.randint(jax.random.fold_in(own, 4), (number_of // 2,), 0, 1 << 20) % (margin + 1)
    sizes = sizes.at[giver].add(-passed).at[taker].add(passed)
    labels = jnp.searchsorted(jnp.cumsum(sizes), jnp.arange(rows * top), side="right").astype(jnp.int32)
    listing = labels.reshape(top, rows).T
    listing = listing[jax.random.permutation(jax.random.fold_in(own, 1), rows)]
    turn = jax.random.randint(jax.random.fold_in(own, 2), (rows, 1), 0, top)
    return jnp.take_along_axis(listing, (jnp.arange(top)[None, :] + turn) % top, axis=1)


def portions_of(count, total, reach, skew, full):
    loads = [(1 << 20) // math.isqrt(rank ** skew) + 1 for rank in range(1, count + 1)]
    largest = reach if full else min(reach, max(-(-total // count), total * loads[0] // sum(loads)))
    least = 1 if total - largest >= count - 1 else 0
    given, surplus = [largest] + [least] * (count - 1), total - largest - least * (count - 1)
    while surplus > 0:
        movable = [i for i in range(1, count) if given[i] < largest] or [i for i in range(1, count) if given[i] < reach]
        pool, left = sum([loads[i] for i in movable]), surplus
        for i in movable:
            more = min(reach - given[i], max(1, left * loads[i] // pool), surplus)
            given[i] = given[i] + more
            surplus = surplus - more
    return np.array(given)


def scatter_about(rng, shape, width, limit, cuts=(), kind=jnp.bfloat16):
    result = jax.random.normal(rng, shape, jnp.float32) * width
    if len(cuts) > 0:
        result = shard_levels(rng, shape, cuts, -0.22, 0.18) * result
    return jnp.clip(result, min=-limit, max=limit).astype(kind)


def setup_inputs(seed: int = 0) -> dict:
    arg_keys = jax.random.split(jax.random.key(seed), 11)
    hidden = scatter_about(arg_keys[0], (ROWS, STEPS, D), 1.0, 6.0, ((0, 64), (2, 4)))
    w_dkv = scatter_about(arg_keys[1], (D, LAT + ROPE), D ** -0.5, 0.0625, ((0, 4),))
    kv_gain = jnp.clip(1.0 + 0.1 * jax.random.normal(arg_keys[2], (LAT,), jnp.float32), 0.5, 1.5)
    q_latent = draw_q_latent(jax.random.fold_in(arg_keys[10], 71), 0)
    q_rope = scatter_about(arg_keys[4], (ROWS, STEPS, HEADS * ROPE), 1.0, 6.0, ((0, 64), (2, 4)))
    w_uv = scatter_about(arg_keys[5], (HEADS, LAT, VH), LAT ** -0.5, 0.25, ((0, 4),))
    latent_cache = draw_latent_cache(jax.random.fold_in(arg_keys[10], 71), 0)
    block_slots = with_ends(ranked(arg_keys[7], (ROWS, NB), BLK_DEV, 2), jax.random.fold_in(arg_keys[7], 3), 0, BLK_DEV - 1).astype(jnp.int32)
    seg_owner_keys = jax.random.split(jax.random.fold_in(arg_keys[8], 1), ROWS // ROWS_DEV)
    seg_owner_turns = jax.random.permutation(jax.random.fold_in(arg_keys[8], 3), ROWS // ROWS_DEV)
    seg_owner = jax.vmap(lambda own, number: shared_out(jax.random.fold_in(arg_keys[8], 2), own, number, ROWS_DEV, N_CACHE, SEGS, CAP, 2))(seg_owner_keys, seg_owner_turns).reshape((ROWS, SEGS))
    lengths = with_ends(jax.random.randint(arg_keys[9], (ROWS,), 1, NB * BT + 1), jax.random.fold_in(arg_keys[9], 1), 1, NB * BT).astype(jnp.int32)
    return {"hidden": hidden, "w_dkv": w_dkv, "kv_gain": kv_gain, "q_latent": q_latent, "q_rope": q_rope, "w_uv": w_uv, "latent_cache": latent_cache, "block_slots": block_slots, "seg_owner": seg_owner, "lengths": lengths}


softmax_scale = 192.0 ** (-0.5)
masked_score = -1e+30
rope_base = 10000.0

def rotate(values, places):
    half_width = values.shape[-1] // 2
    frequency = rope_base ** (-(jnp.arange(half_width, dtype=jnp.float32) * 2.0 / values.shape[-1]))
    angles = places.astype(jnp.float32)[..., None] * frequency
    cosine = jnp.cos(angles)
    sine_part = jnp.sin(angles)
    front_half = values[..., :half_width]
    back_half = values[..., half_width:]
    return jnp.concatenate([front_half * cosine - back_half * sine_part, front_half * sine_part + back_half * cosine], -1)

def finish_latent(summed, places, kv_gain):
    latent = summed[..., :LAT]
    normed = latent * lax.rsqrt(lax.optimization_barrier(jnp.mean(latent * latent, -1, keepdims=True)) + 1e-06) * kv_gain
    return jnp.concatenate([normed, rotate(summed[..., LAT:], places)], -1).astype(jnp.bfloat16)

def reference(hidden, w_dkv, kv_gain, q_latent, q_rope, w_uv, latent_cache, block_slots, seg_owner, lengths):
    channels = LAT + ROPE
    positions = lengths[:, None] + jnp.arange(STEPS, dtype=jnp.int32)[None, :]
    summed = jnp.dot(hidden.reshape(ROWS * STEPS, D), w_dkv, preferred_element_type=jnp.float32)
    new_latent = finish_latent(summed.reshape(ROWS, STEPS, channels), positions, kv_gain)
    seg_blocks = NB // SEGS
    token_span = seg_blocks * BT
    query_count = STEPS * HEADS
    w_uv_full = w_uv.astype(jnp.float32)

    def per_row(operands):
        lat_row, rope_row, owners, slots, length, places, fresh = operands
        roped = rotate(rope_row.reshape(STEPS, HEADS, ROPE).astype(jnp.float32), places[:, None]).astype(jnp.bfloat16)
        queries = jnp.concatenate([lat_row.reshape(STEPS, HEADS, LAT), roped], -1)
        queries = queries.astype(jnp.float32).reshape(query_count, channels)
        block_ids = (jnp.repeat(owners, seg_blocks) * BLK_DEV + slots).astype(jnp.int32)
        tokens_kv = latent_cache[block_ids].astype(jnp.float32).reshape(SEGS, token_span, channels)
        scores = jnp.einsum('qc,ktc->kqt', queries, tokens_kv) * softmax_scale
        token_places = jnp.arange(SEGS, dtype=jnp.int32)[:, None] * token_span + jnp.arange(token_span, dtype=jnp.int32)[None, :]
        living = (token_places < length)[:, None, :]
        masked = jnp.where(living, scores, masked_score)
        highest = lax.optimization_barrier(jnp.max(masked, -1))
        weights = jnp.where(living, jnp.exp(masked - highest[..., None]), 0.0)
        totals = lax.optimization_barrier(jnp.sum(weights, -1))
        rounded = lax.optimization_barrier(weights.astype(jnp.bfloat16)).astype(jnp.float32)
        seg_sum = jnp.einsum('kqt,ktl->kql', rounded, tokens_kv[..., :LAT])
        seg_b = lax.optimization_barrier(seg_sum.astype(jnp.bfloat16)).astype(jnp.float32)
        projected = jnp.einsum('kshl,hlv->kshv', seg_b.reshape(SEGS, STEPS, HEADS, LAT), w_uv_full)
        projected = projected.reshape(SEGS, query_count, VH)
        fresh_full = fresh.astype(jnp.float32)
        own_scores = jnp.einsum('qc,tc->qt', queries, fresh_full) * softmax_scale
        causal = jnp.arange(STEPS)[None, :] <= (jnp.arange(query_count) // HEADS)[:, None]
        own_masked = jnp.where(causal, own_scores, masked_score)
        own_top = lax.optimization_barrier(jnp.max(own_masked, -1))
        own_weights = jnp.where(causal, jnp.exp(own_masked - own_top[:, None]), 0.0)
        own_total = lax.optimization_barrier(jnp.sum(own_weights, -1))
        own_sum = jnp.dot(own_weights, fresh_full[:, :LAT])
        own_b = lax.optimization_barrier(own_sum.astype(jnp.bfloat16)).astype(jnp.float32)
        own_proj = jnp.einsum('shl,hlv->shv', own_b.reshape(STEPS, HEADS, LAT), w_uv_full).reshape(query_count, VH)
        largest = jnp.maximum(own_top, lax.optimization_barrier(jnp.max(highest, 0)))
        factor = jnp.exp(highest - largest[None, :])
        own_factor = jnp.exp(own_top - largest)
        numerator = lax.optimization_barrier(jnp.sum(factor[..., None] * projected, 0)) + own_factor[:, None] * own_proj
        denominator = lax.optimization_barrier(jnp.sum(factor * totals, 0)) + own_factor * own_total
        heads_out = numerator / denominator[:, None]
        return heads_out.astype(jnp.bfloat16).reshape(STEPS, HEADS * VH)
    attn_out = lax.map(per_row, (q_latent, q_rope, seg_owner, block_slots, lengths, positions, new_latent))
    return (attn_out, new_latent)
```

```python
import functools

import jax
import jax.numpy as jnp
from jax import lax
from jax.experimental import pallas as pl
from jax.experimental.pallas import tpu as pltpu
from jax.sharding import PartitionSpec as P

LAT = 512
SEGS = 8
NY, NZ, NC, NX = 4, 8, 2, 4
GROUP = NZ * NC
WIDE = 640
QUARTER = 16

softmax_scale = 192.0 ** (-0.5)
masked_score = -1e30
rope_base = 10000.0


def place(y, z, c):
    return (y % NY * NZ + z % NZ) * NC + c


def spots():
    return [(y, z, c) for y in range(NY) for z in range(NZ) for c in range(NC)]


def along_y(array, by):
    return lax.ppermute(
        array, "cache", [(place(y, z, c), place(y + by, z, c)) for y, z, c in spots()]
    )


def along_x(array, by):
    return lax.ppermute(array, "tensor", [(i, (i + by) % NX) for i in range(NX)])


def other_core(array):
    return lax.ppermute(
        array, "cache", [(place(y, z, c), place(y, z, 1 - c)) for y, z, c in spots()]
    )


def rotate(values, places):
    half_width = values.shape[-1] // 2
    frequency = rope_base ** (-(jnp.arange(half_width, dtype=jnp.float32) * 2.0 / values.shape[-1]))
    angles = places.astype(jnp.float32)[..., None] * frequency
    cosine = jnp.cos(angles)
    sine_part = jnp.sin(angles)
    front_half = values[..., :half_width]
    back_half = values[..., half_width:]
    return jnp.concatenate(
        [front_half * cosine - back_half * sine_part, front_half * sine_part + back_half * cosine],
        -1,
    )


def finish_latent(summed, places, kv_gain):
    latent = summed[..., :LAT]
    normed = latent * lax.rsqrt(jnp.mean(latent * latent, -1, keepdims=True) + 1e-06) * kv_gain
    return jnp.concatenate([normed, rotate(summed[..., LAT:], places)], -1).astype(jnp.bfloat16)


def attend_kernel(owners, pieces, prior, *refs):
    blk_ref, live_ref, par_ref = refs[:3]
    refs = refs[3:]
    q_ref, w_ref = refs[:2]
    refs = refs[2:]
    count = len(pieces)
    kv_in = refs[:count]
    refs = refs[count:]
    if prior:
        p_ref, plse_ref = refs[:2]
        refs = refs[2:]
    out_ref, lse_ref, kv, acc, top, total, items, sems = refs
    rows = q_ref.shape[0]
    g = pl.program_id(0)

    @pl.when(g == 0)
    def _():
        parity = par_ref[0]
        copies = []
        for n, (owner, kind, blocks) in enumerate(pieces):
            if kind == "all":
                first = owner * 64
            else:
                side = parity if kind in "AB" else 1 - parity
                first = owner * 64 + side * 32 + (QUARTER if kind in "BR" else 0)
            copies.append(pltpu.make_async_copy(kv_in[n], kv.at[pl.ds(first, blocks)], sems.at[n]))
        for copy in copies:
            copy.start()
        for copy in copies:
            copy.wait()

    acc[...] = jnp.zeros_like(acc)
    top[...] = jnp.full_like(top, masked_score)
    total[...] = jnp.zeros_like(total)
    first = g * (owners * rows)

    def scan(i, n):
        items[n] = first + i
        return n + (live_ref[first + i] > 0).astype(jnp.int32)

    found = lax.fori_loop(0, owners * rows, scan, jnp.int32(0))

    def one(item, live):
        row = item & (rows - 1)
        owner = item // rows - g * owners
        q = q_ref[row]
        blocks = [owner * 64 + blk_ref[item * 8 + t] for t in range(8)]
        scores = []
        for h in range(2):
            keys = jnp.concatenate([kv[b] for b in blocks[4 * h : 4 * h + 4]], 0)
            scores.append(
                lax.dot_general(
                    q, keys, (((1,), (1,)), ((), ())), preferred_element_type=jnp.float32
                )
            )
        score = jnp.concatenate(scores, 1) * softmax_scale
        alive = lax.broadcasted_iota(jnp.int32, score.shape, 1) < live
        masked = jnp.where(alive, score, masked_score)
        highest = jnp.max(masked, 1, keepdims=True)
        weights = jnp.where(alive, jnp.exp(masked - highest), 0.0)
        summed = jnp.sum(weights, 1, keepdims=True)
        weights_b = weights.astype(jnp.bfloat16)
        result = None
        for h in range(2):
            vals = jnp.concatenate([kv[b, :, :LAT] for b in blocks[4 * h : 4 * h + 4]], 0)
            part = jnp.dot(
                weights_b[:, 256 * h : 256 * h + 256], vals, preferred_element_type=jnp.float32
            )
            result = part if result is None else result + part
        return row, highest, summed, result

    def merge(row, highest, summed, result):
        before = top[row]
        now = jnp.maximum(before, highest)
        keep = jnp.exp(before - now)
        add = jnp.exp(highest - now)
        top[row] = now
        total[row] = total[row] * keep + summed * add
        acc[row] = acc[row] * keep[:, :1] + result * add[:, :1]

    def pair(j, carry):
        first_item = items[2 * j]
        second_item = items[jnp.minimum(2 * j + 1, found - 1)]
        second_live = jnp.where(2 * j + 1 < found, live_ref[second_item], 0)
        one_result = one(first_item, live_ref[first_item])
        two_result = one(second_item, second_live)
        merge(*one_result)
        merge(*two_result)
        return carry

    lax.fori_loop(0, (found + 1) // 2, pair, 0)

    sums = total[...]
    has = sums > 0.0
    inverse = jnp.where(has, 1.0 / jnp.where(has, sums, 1.0), 0.0)
    lse = jnp.where(has, top[...] + jnp.log(jnp.where(has, sums, 1.0)), masked_score)
    total[...] = inverse
    if prior:
        earlier = plse_ref[...]
        most = jnp.maximum(lse, earlier)
        w_new = jnp.exp(lse - most)
        w_old = jnp.exp(earlier - most)
        both = w_new + w_old
        top[...] = w_new / both
        lse = most + jnp.log(both)
        diagonal = lax.broadcasted_iota(jnp.int32, lse.shape, 1) == lax.broadcasted_iota(
            jnp.int32, lse.shape, 2
        )
        lse_ref[...] = jnp.sum(jnp.where(diagonal, lse, 0.0), 1)
    else:
        lse_ref[...] = lse
    for j in range(8):
        span = slice(8 * j, 8 * j + 8)
        x = acc[:, span, :] * total[:, span, :1]
        x = x.reshape(rows * 8, LAT).astype(jnp.bfloat16)
        y = jnp.dot(x, w_ref[j], preferred_element_type=jnp.float32)
        upper = (lax.broadcasted_iota(jnp.int32, (rows * 8, 128), 0) & 7) < 4
        y = jnp.where(upper, y[:, :128], y[:, 128:]).reshape(rows, 8, 128)
        if prior:
            w_new = top[:, span, :]
            y = y * w_new + p_ref[:, span, :] * (1.0 - w_new)
        out_ref[:, span, :] = y.astype(out_ref.dtype)


def attend(queries, w_pairs, blocks, live, parity, arrays, pieces, owners, earlier=None):
    total_rows = queries.shape[0]
    half = total_rows // 2
    prior = earlier is not None
    row_block = lambda *tail: pl.BlockSpec(
        (half,) + tail, lambda g, *_: (g,) + (0,) * len(tail)
    )
    in_specs = [
        row_block(64, WIDE),
        pl.BlockSpec(w_pairs.shape, lambda g, *_: (0, 0, 0)),
    ] + [pl.BlockSpec(memory_space=pl.ANY)] * len(arrays)
    operands = [queries, w_pairs, *arrays]
    if prior:
        in_specs += [row_block(64, 128), row_block(64, 128)]
        operands += list(earlier)
        out_shape = [
            jax.ShapeDtypeStruct((total_rows, 64, 128), jnp.bfloat16),
            jax.ShapeDtypeStruct((total_rows, 128), jnp.float32),
        ]
        out_specs = [row_block(64, 128), row_block(128)]
    else:
        out_shape = [
            jax.ShapeDtypeStruct((total_rows, 64, 128), jnp.float32),
            jax.ShapeDtypeStruct((total_rows, 64, 128), jnp.float32),
        ]
        out_specs = [row_block(64, 128), row_block(64, 128)]
    return pl.pallas_call(
        functools.partial(attend_kernel, owners, pieces, prior),
        out_shape=out_shape,
        grid_spec=pltpu.PrefetchScalarGridSpec(
            num_scalar_prefetch=3,
            grid=(2,),
            in_specs=in_specs,
            out_specs=out_specs,
            scratch_shapes=[
                pltpu.VMEM((owners * 64, 64, WIDE), jnp.bfloat16),
                pltpu.VMEM((half, 64, LAT), jnp.float32),
                pltpu.VMEM((half, 64, 128), jnp.float32),
                pltpu.VMEM((half, 64, 128), jnp.float32),
                pltpu.SMEM((owners * half,), jnp.int32),
                pltpu.SemaphoreType.DMA((len(arrays),)),
            ],
        ),
        compiler_params=pltpu.CompilerParams(vmem_limit_bytes=58 * 1024 * 1024),
        cost_estimate=pl.CostEstimate(
            flops=owners * 32 * 64 * 512 * 1088 * 2,
            bytes_accessed=owners * 5 * 2**20 + 2**24,
            transcendentals=owners * 32 * 64 * 512,
        ),
    )(blocks, live, parity, *operands)


def tables(info, targets, half):
    slots = info[:, 0, :]
    owners = info[:, 1, :SEGS]
    lengths = info[:, 1, SEGS] * 64 + info[:, 1, SEGS + 1]
    rows = info.shape[0]
    segment = jnp.arange(SEGS, dtype=jnp.int32)
    match = (owners[None] == targets[:, None, None]).astype(jnp.int32)
    tokens = jnp.clip(lengths[:, None] - segment[None, :] * 512, 0, 512)
    live = jnp.sum(match * tokens[None], -1)
    blocks = jnp.sum(match[..., None] * slots.reshape(rows, SEGS, SEGS)[None], 2)
    count = targets.shape[0]
    live = live.reshape(count, 2, half).swapaxes(0, 1).reshape(-1)
    blocks = blocks.reshape(count, 2, half, SEGS).swapaxes(0, 1).reshape(-1)
    return blocks, live


def body(
    hidden, w_dkv, kv_gain, q_latent, q_rope, w_uv, latent_cache, block_slots, seg_owner, lengths
):
    row_count, step_count = hidden.shape[:2]
    channels = latent_cache.shape[-1]
    heads_dev = q_latent.shape[2] // LAT
    rope_width = channels - LAT
    me = lax.axis_index("cache")
    core = me % NC
    y_here = me // GROUP
    parity = lax.axis_index("tensor") % 2
    positions = lengths[:, None] + jnp.arange(step_count, dtype=jnp.int32)[None, :]

    roped = rotate(
        q_rope.reshape(row_count, step_count, heads_dev, rope_width).astype(jnp.float32),
        positions[..., None],
    ).astype(jnp.bfloat16)
    queries = jnp.concatenate(
        [q_latent.reshape(row_count, step_count, heads_dev, LAT), roped], -1
    ).swapaxes(1, 2)
    queries = queries.reshape(row_count, heads_dev * step_count, channels)
    second = jnp.concatenate([seg_owner, lengths[:, None] // 64, lengths[:, None] % 64], 1)
    second = jnp.pad(second, ((0, 0), (0, 64 - second.shape[1])))
    info = jnp.stack([block_slots, second], 1).astype(jnp.bfloat16)
    info = jnp.pad(info, ((0, 0), (0, heads_dev * step_count - 2), (0, 0)))
    message = jnp.concatenate([queries, info], -1)
    all_queries = lax.all_gather(
        message,
        "cache",
        axis=0,
        tiled=True,
        axis_index_groups=[[y * GROUP + i for i in range(GROUP)] for y in range(NY)],
    )

    held = jnp.pad(latent_cache, ((0, 0), (0, 0), (0, WIDE - channels)))
    half_a = lax.dynamic_slice_in_dim(held, parity * 32, QUARTER, 0)
    half_b = lax.dynamic_slice_in_dim(held, parity * 32 + QUARTER, QUARTER, 0)
    m_a = along_y(half_a, 1)
    p_b = along_y(half_b, -1)
    m_b = along_y(half_b, 1)
    p_a = along_y(half_a, -1)
    m_l = along_x(m_a, 1)
    p_r = along_x(p_b, -1)
    t_a = along_y(m_a, 1)
    t_b = along_y(p_b, -1)
    m_r = along_x(m_b, -1)
    p_l = along_x(p_a, 1)
    t_l = along_x(t_a, 1)
    t_r = along_x(t_b, -1)

    partial_sum = jnp.einsum("rsd,dc->rsc", hidden, w_dkv, preferred_element_type=jnp.float32)
    summed = lax.psum(partial_sum, "tensor")
    new_latent = finish_latent(summed, positions, kv_gain)
    own_scores = (
        jnp.einsum("rqc,rtc->rqt", queries, new_latent, preferred_element_type=jnp.float32)
        * softmax_scale
    )
    steps_of = jnp.arange(heads_dev * step_count) % step_count
    causal = (jnp.arange(step_count)[None, :] <= steps_of[:, None])[None]
    own_masked = jnp.where(causal, own_scores, masked_score)
    own_top = jnp.max(own_masked, -1)
    own_weights = jnp.where(causal, jnp.exp(own_masked - own_top[..., None]), 0.0)
    own_total = jnp.sum(own_weights, -1)
    own_sum = jnp.einsum("rqt,rtl->rql", own_weights, new_latent[..., :LAT].astype(jnp.float32))
    own_b = own_sum.astype(jnp.bfloat16).reshape(row_count, heads_dev, step_count, LAT)
    own_proj = jnp.einsum("rhsl,hlv->rhsv", own_b, w_uv, preferred_element_type=jnp.float32)
    own_proj = own_proj.reshape(row_count, heads_dev * step_count, -1)
    own_part = own_proj / own_total[..., None]
    own_lse = own_top + jnp.log(own_total)

    w_pairs = w_uv.reshape(heads_dev // 2, 2, LAT, -1).swapaxes(1, 2)
    w_pairs = w_pairs.reshape(heads_dev // 2, LAT, -1)
    table = all_queries[:, :2, channels:].astype(jnp.float32).astype(jnp.int32)
    offsets = jnp.array([0, NY - 1, 1, 2], jnp.int32)
    targets = (y_here + offsets) % NY * GROUP + me % GROUP
    half = all_queries.shape[0] // 2
    parities = parity[None].astype(jnp.int32)
    near_pieces = [(0, "all", 64)]
    near_arrays = [held]
    for owner, arrays in ((1, (m_a, m_b, m_l, m_r)), (2, (p_a, p_b, p_l, p_r))):
        near_pieces += [(owner, kind, QUARTER) for kind in "ABLR"]
        near_arrays += arrays
    blocks, live = tables(table, targets[:3], half)
    near = attend(
        all_queries, w_pairs, blocks, live, parities, near_arrays, near_pieces, 3
    )
    blocks, live = tables(table, targets[3:], half)
    far_pieces = [(0, kind, QUARTER) for kind in "ABLR"]
    part, lse = attend(
        all_queries, w_pairs, blocks, live, parities, (t_a, t_b, t_l, t_r), far_pieces, 1, near
    )

    width = part.shape[1]
    part = part.reshape(NZ, NC, row_count, width, -1)
    lse = lse[:, :width].reshape(NZ, NC, row_count, width)
    pick = lambda array, which: lax.dynamic_index_in_dim(array, which, 1, keepdims=False)
    mine, theirs = pick(part, core), other_core(pick(part, 1 - core))
    lse_mine, lse_theirs = pick(lse, core), other_core(pick(lse, 1 - core))
    most = jnp.maximum(lse_mine, lse_theirs)
    w_mine, w_theirs = jnp.exp(lse_mine - most), jnp.exp(lse_theirs - most)
    both = w_mine + w_theirs
    chip_part = mine * (w_mine / both)[..., None] + theirs * (w_theirs / both)[..., None]
    chip_part = chip_part.astype(jnp.bfloat16)
    chip_lse = most + jnp.log(both)
    along_z = [[place(y, z, c) for z in range(NZ)] for y in range(NY) for c in range(NC)]
    exchange = lambda array: lax.all_to_all(
        array, "cache", split_axis=0, concat_axis=0, axis_index_groups=along_z, tiled=True
    )
    home_part = exchange(chip_part)
    home_lse = exchange(chip_lse)
    largest = jnp.maximum(own_lse, jnp.max(home_lse, 0))
    factor = jnp.exp(home_lse - largest[None])
    own_factor = jnp.exp(own_lse - largest)
    numerator = jnp.sum(factor[..., None] * home_part, 0) + own_factor[..., None] * own_part
    denominator = jnp.sum(factor, 0) + own_factor
    attn_out = (numerator / denominator[..., None]).astype(jnp.bfloat16)
    attn_out = attn_out.reshape(row_count, heads_dev, step_count, -1).swapaxes(1, 2)
    return (attn_out.reshape(row_count, step_count, -1), new_latent)


def solution(mesh):
    in_specs = (
        P("cache", None, "tensor"),
        P("tensor", None),
        P(),
        P("cache", None, "tensor"),
        P("cache", None, "tensor"),
        P("tensor", None, None),
        P("cache", None, None),
        P("cache", None),
        P("cache", None),
        P("cache"),
    )
    out_specs = (P("cache", None, "tensor"), P("cache", None, None))
    return jax.shard_map(body, mesh=mesh, in_specs=in_specs, out_specs=out_specs, check_vma=False)
```

```python
import functools

import jax
import jax.numpy as jnp
from jax import lax
from jax.experimental import pallas as pl
from jax.experimental.pallas import tpu as pltpu
from jax.sharding import PartitionSpec as P

LAT = 512
SEGS = 8
NY, NZ, NC, NX = 4, 8, 2, 4
GROUP = NZ * NC
WIDE = 640
AT_ONCE = 4
PAIRS = 8
VMEM_BYTES = 60 * 1024 * 1024

softmax_scale = 192.0 ** (-0.5)
masked_score = -1e30
rope_base = 10000.0


def place(y, z, c):
    return (y % NY * NZ + z % NZ) * NC + c


def spots():
    return [(y, z, c) for y in range(NY) for z in range(NZ) for c in range(NC)]


def along_y(array, by):
    return lax.ppermute(
        array, "cache", [(place(y, z, c), place(y + by, z, c)) for y, z, c in spots()]
    )


def along_x(array, by):
    return lax.ppermute(array, "tensor", [(i, (i + by) % NX) for i in range(NX)])


def other_core(array):
    return lax.ppermute(
        array, "cache", [(place(y, z, c), place(y, z, 1 - c)) for y, z, c in spots()]
    )


def angle_tables(places, width):
    half_width = width // 2
    frequency = rope_base ** (-(jnp.arange(half_width, dtype=jnp.float32) * 2.0 / width))
    angles = places.astype(jnp.float32)[..., None] * frequency
    return lax.optimization_barrier((jnp.cos(angles), jnp.sin(angles)))


def rotate(values, cosine, sine_part):
    half_width = values.shape[-1] // 2
    front_half = values[..., :half_width]
    back_half = values[..., half_width:]
    return jnp.concatenate(
        [front_half * cosine - back_half * sine_part, front_half * sine_part + back_half * cosine],
        -1,
    )


def finish_latent(summed, cosine, sine_part, kv_gain):
    latent = summed[..., :LAT]
    normed = latent * lax.rsqrt(jnp.mean(latent * latent, -1, keepdims=True) + 1e-06) * kv_gain
    roped = rotate(summed[..., LAT:], cosine, sine_part)
    return jnp.concatenate([normed, roped], -1).astype(jnp.bfloat16)


def gate(*arrays):
    anywhere = pl.BlockSpec(memory_space=pltpu.HBM)
    return pl.pallas_call(
        lambda *refs: None,
        out_shape=[jax.ShapeDtypeStruct(a.shape, a.dtype) for a in arrays],
        in_specs=[anywhere] * len(arrays),
        out_specs=[anywhere] * len(arrays),
        input_output_aliases={i: i for i in range(len(arrays))},
        compiler_params=pltpu.CompilerParams(vmem_limit_bytes=VMEM_BYTES),
    )(*arrays)


def pack_kernel(par_ref, len_in, cache, out_a, out_b, len_out, held, sem):
    copy = pltpu.make_async_copy(cache.at[pl.ds(par_ref[0] * 32, 32)], held, sem)
    copy.start()
    for row in range(len_in.shape[0]):
        len_out[row] = len_in[row]
    copy.wait()
    for quarter, out in enumerate((out_a, out_b)):

        def one(pair, carry):
            ropes = []
            for b in range(2):
                block = held[quarter * 2 * PAIRS + 2 * pair + b]
                out[pair, 64 * b : 64 * b + 64, :] = block[:, :LAT]
                rope = block[:, LAT:]
                rope = jnp.concatenate([rope[:32], rope[32:]], 1)
                ropes += [rope[:16], rope[16:]]
            out[pair, 128:, :] = jnp.concatenate(ropes, 1)
            return carry

        lax.fori_loop(0, PAIRS, one, 0)


def pack(latent_cache, parity, lengths):
    shape = jax.ShapeDtypeStruct((PAIRS, 144, LAT), latent_cache.dtype)
    return pl.pallas_call(
        pack_kernel,
        out_shape=[shape, shape, jax.ShapeDtypeStruct(lengths.shape, lengths.dtype)],
        grid_spec=pltpu.PrefetchScalarGridSpec(
            num_scalar_prefetch=2,
            grid=(),
            in_specs=[pl.BlockSpec(memory_space=pl.ANY)],
            out_specs=[pl.BlockSpec(memory_space=pltpu.VMEM)] * 2
            + [pl.BlockSpec(memory_space=pltpu.SMEM)],
            scratch_shapes=[
                pltpu.VMEM((32,) + latent_cache.shape[1:], latent_cache.dtype),
                pltpu.SemaphoreType.DMA,
            ],
        ),
        compiler_params=pltpu.CompilerParams(vmem_limit_bytes=VMEM_BYTES),
    )(parity, lengths, latent_cache)


def attend_kernel(owners, pieces, unused, stage, *refs):
    blk_ref, live_ref, par_ref, q_in, w_ref = refs[:5]
    refs = refs[5:]
    kv_in = refs[: len(pieces)]
    refs = refs[len(pieces) + unused :]
    if stage != "first":
        state_in, lse_in = refs[:2]
        refs = refs[2:]
    state, lse_ref, kv, queries, normal, slot_lse, projected, items, kv_sems, q_sems, row_sems = refs
    rows = lse_ref.shape[0]

    copies = [[] for _ in range(owners)]
    for n, (owner, side, offset) in enumerate(pieces):
        first = owner * 4 * PAIRS + offset
        if side == "mine":
            first = first + par_ref[0] * 2 * PAIRS
        elif side == "other":
            first = first + (1 - par_ref[0]) * 2 * PAIRS
        copies[owner].append(
            pltpu.make_async_copy(
                kv_in[n], kv.at[pl.ds(first, kv_in[n].shape[0])], kv_sems.at[n]
            )
        )
    for some in copies:
        for copy in some:
            copy.start()
    if stage == "middle":
        whole = pltpu.make_async_copy(state_in, state, row_sems.at[0])
        whole.start()

    def scan(i, n):
        items[n] = i
        return n + (live_ref[i] > 0).astype(jnp.int32)

    ends = [jnp.int32(0)]
    for o in range(owners):
        ends.append(lax.fori_loop(o * rows, (o + 1) * rows, scan, ends[-1], unroll=8))
    found = ends[-1]

    def row_of(slot):
        return items[slot] & (rows - 1)

    def fetch(slot):
        return pltpu.make_async_copy(q_in.at[row_of(slot)], queries.at[slot], q_sems.at[slot])

    def load_row(slot):
        return pltpu.make_async_copy(state.at[row_of(slot)], normal.at[slot, :, :128], row_sems.at[slot])

    def store_row(slot):
        return pltpu.make_async_copy(projected.at[slot], state.at[row_of(slot)], row_sems.at[slot])

    def each(action):
        def step(slot, carry):
            action(slot)
            return carry

        lax.fori_loop(0, found, step, 0)

    each(lambda slot: fetch(slot).start())
    if stage == "first":
        state[...] = jnp.zeros_like(state)
        lse_ref[...] = jnp.full_like(lse_ref, masked_score)
    else:
        lse_ref[...] = lse_in[...]

    low_lanes = lax.broadcasted_iota(jnp.int32, (16, 128), 1) < 64

    def blocks_of(slot):
        item = items[slot]
        return [(item // rows) * 64 + blk_ref[item * 8 + t] for t in range(8)]

    def latents(b):
        if stage == "first":
            return kv[b, :, :LAT]
        return kv[b // 2, pl.ds(pl.multiple_of((b & 1) * 64, 64), 64), :]

    def keys(b):
        if stage == "first":
            return kv[b]
        some = kv[b // 2, 128:, pl.ds(pl.multiple_of((b & 1) * 256, 256), 256)]
        nothing = jnp.zeros((16, 128), some.dtype)
        groups = [some[:, :128], some[:, 128:]]
        ropes = [jnp.where(low_lanes, g, nothing) for g in groups]
        ropes += [jnp.where(low_lanes, nothing, g) for g in groups]
        return jnp.concatenate([latents(b), jnp.concatenate(ropes, 0)], 1)

    def score_of(slot, blocks):
        q = queries[slot]
        channels = LAT + 64
        q = q[:, :channels]
        if stage != "first":
            q = jnp.concatenate([q, q[:, LAT:]], 1)
        scores = []
        for h in range(2):
            some = jnp.concatenate([keys(b) for b in blocks[4 * h : 4 * h + 4]], 0)
            scores.append(
                lax.dot_general(
                    q, some, (((1,), (1,)), ((), ())), preferred_element_type=jnp.float32
                )
            )
        return jnp.concatenate(scores, 1) * softmax_scale

    def soften(score, live):
        alive = lax.broadcasted_iota(jnp.int32, score.shape, 1) < live
        masked = jnp.where(alive, score, masked_score)
        highest = jnp.max(masked, 1, keepdims=True)
        weights = jnp.where(alive, jnp.exp(masked - highest), 0.0)
        summed = jnp.sum(weights, 1, keepdims=True)
        return weights.astype(jnp.bfloat16), 1.0 / summed, highest + jnp.log(summed)

    def value_of(weights_b, blocks):
        result = None
        for h in range(2):
            vals = jnp.concatenate([latents(b) for b in blocks[4 * h : 4 * h + 4]], 0)
            part = jnp.dot(
                weights_b[:, 256 * h : 256 * h + 256], vals, preferred_element_type=jnp.float32
            )
            result = part if result is None else result + part
        return result

    for o in range(owners):
        begin, end = ends[o], ends[o + 1]
        for copy in copies[o]:
            copy.wait()

        def several(j, carry):
            first = begin + AT_ONCE * j
            group = [jnp.minimum(first + i, end - 1) for i in range(AT_ONCE)]
            for i, slot in enumerate(group):

                @pl.when(first + i < end)
                def _():
                    fetch(slot).wait()

            blocks = [blocks_of(slot) for slot in group]
            scores = [score_of(slot, some) for slot, some in zip(group, blocks)]
            soft = [soften(score, live_ref[items[slot]]) for score, slot in zip(scores, group)]
            results = [value_of(one[0], some) for one, some in zip(soft, blocks)]
            for slot, one, result in zip(group, soft, results):
                normal[slot] = result * one[1]
                slot_lse[slot] = jnp.broadcast_to(one[2], slot_lse.shape[1:])
            return carry

        lax.fori_loop(0, (end - begin + AT_ONCE - 1) // AT_ONCE, several, 0)

    def project(group, carry):
        some = pl.ds(pl.multiple_of(group * 32, 32), 32)
        for j in range(8):
            span = slice(8 * j, 8 * j + 8)
            x = normal[some, span, :].reshape(32 * 8, LAT).astype(jnp.bfloat16)
            w = jnp.concatenate([w_ref[2 * j], w_ref[2 * j + 1]], 1)
            y = jnp.dot(x, w, preferred_element_type=jnp.float32)
            upper = (lax.broadcasted_iota(jnp.int32, (32 * 8, 128), 0) & 7) < 4
            projected[some, span, :] = jnp.where(upper, y[:, :128], y[:, 128:]).reshape(32, 8, 128)
        return carry

    lax.fori_loop(0, (found + 31) // 32, project, 0)
    if stage == "middle":
        whole.wait()
    if stage == "last":
        each(lambda slot: load_row(slot).start())
        each(lambda slot: load_row(slot).wait())

    diagonal = lax.broadcasted_iota(jnp.int32, (64, 128), 0) == lax.broadcasted_iota(
        jnp.int32, (64, 128), 1
    )
    for o in range(owners):
        begin, end = ends[o], ends[o + 1]

        def merge(j, carry):
            group = [jnp.minimum(begin + AT_ONCE * j + i, end - 1) for i in range(AT_ONCE)]
            where = [row_of(slot) for slot in group]
            values = []
            for slot, row in zip(group, where):
                across = jnp.broadcast_to(lse_ref[pl.ds(row, 1), :], (64, 128))
                before = jnp.sum(jnp.where(diagonal, across, 0.0), 1, keepdims=True)
                added = slot_lse[slot]
                most = jnp.maximum(before, added)
                keep = jnp.exp(before - most)
                add = jnp.exp(added - most)
                both = keep + add
                lse = most + jnp.log(both)
                lse_row = jnp.sum(jnp.where(diagonal, lse, 0.0), 0, keepdims=True)
                old = normal[slot, :, :128] if stage == "last" else state[row]
                values.append((lse_row, (old * keep + projected[slot] * add) / both))
            for slot, row, (lse_row, value) in zip(group, where, values):
                lse_ref[pl.ds(row, 1), :] = lse_row
                if stage == "last":
                    projected[slot] = value
                else:
                    state[row] = value
            return carry

        lax.fori_loop(0, (end - begin + AT_ONCE - 1) // AT_ONCE, merge, 0)
    if stage == "last":
        each(lambda slot: store_row(slot).start())
        each(lambda slot: store_row(slot).wait())


def attend(queries, w_uv, blocks, live, parity, arrays, pieces, owners, stage, after, earlier):
    rows = queries.shape[0]
    slots = owners * GROUP * 2
    all_blocks = (owners * 64,) if stage == "first" else (owners * 4 * PAIRS,)
    whole = pl.BlockSpec(memory_space=pltpu.VMEM)
    anywhere = pl.BlockSpec(memory_space=pltpu.HBM)
    in_specs = [anywhere, whole] + [anywhere] * len(arrays)
    in_specs += [anywhere] * len(after)
    operands = [queries, w_uv, *arrays, *after, *earlier]
    if earlier:
        in_specs += [anywhere, whole]
    return pl.pallas_call(
        functools.partial(attend_kernel, owners, pieces, len(after), stage),
        out_shape=[
            jax.ShapeDtypeStruct((rows, 64, 128), jnp.float32),
            jax.ShapeDtypeStruct((rows, 128), jnp.float32),
        ],
        grid_spec=pltpu.PrefetchScalarGridSpec(
            num_scalar_prefetch=3,
            grid=(),
            in_specs=in_specs,
            out_specs=[anywhere if stage == "last" else whole, whole],
            scratch_shapes=[
                pltpu.VMEM(all_blocks + arrays[0].shape[1:], jnp.bfloat16),
                pltpu.VMEM((slots, 64, WIDE), jnp.bfloat16),
                pltpu.VMEM((slots, 64, LAT), jnp.float32),
                pltpu.VMEM((slots, 64, 128), jnp.float32),
                pltpu.VMEM((slots, 64, 128), jnp.float32),
                pltpu.SMEM((owners * rows,), jnp.int32),
                pltpu.SemaphoreType.DMA((len(arrays),)),
                pltpu.SemaphoreType.DMA((slots,)),
                pltpu.SemaphoreType.DMA((slots,)),
            ],
        ),
        input_output_aliases={3 + len(operands) - 2: 0} if stage == "last" else {},
        compiler_params=pltpu.CompilerParams(vmem_limit_bytes=VMEM_BYTES),
        cost_estimate=pl.CostEstimate(
            flops=owners * 32 * 64 * 512 * 1088 * 2,
            bytes_accessed=owners * 5 * 2**20 + 2**24,
            transcendentals=owners * 32 * 64 * 512,
        ),
    )(blocks, live, parity, *operands)


def tables(info, targets):
    slots = info[:, 0, :]
    owners = info[:, 1, :SEGS]
    lengths = info[:, 1, SEGS] * 64 + info[:, 1, SEGS + 1]
    rows = info.shape[0]
    segment = jnp.arange(SEGS, dtype=jnp.int32)
    match = (owners[None] == targets[:, None, None]).astype(jnp.int32)
    tokens = jnp.clip(lengths[:, None] - segment[None, :] * 512, 0, 512)
    live = jnp.sum(match * tokens[None], -1)
    blocks = jnp.sum(match[..., None] * slots.reshape(rows, SEGS, SEGS)[None], 2)
    return blocks.reshape(-1), live.reshape(-1)


def body(
    hidden, w_dkv, kv_gain, q_latent, q_rope, w_uv, latent_cache, block_slots, seg_owner, lengths
):
    row_count, step_count = hidden.shape[:2]
    channels = latent_cache.shape[-1]
    heads_dev = q_latent.shape[2] // LAT
    rope_width = channels - LAT
    me = lax.axis_index("cache")
    core = me % NC
    y_here = me // GROUP
    parity = lax.axis_index("tensor") % 2
    parities = parity.astype(jnp.int32)[None]
    half_a, half_b, lengths = pack(latent_cache, parities, lengths)
    positions = lengths[:, None] + jnp.arange(step_count, dtype=jnp.int32)[None, :]

    cosine, sine_part = angle_tables(positions, rope_width)

    roped = rotate(
        q_rope.reshape(row_count, step_count, heads_dev, rope_width).astype(jnp.float32),
        cosine[:, :, None],
        sine_part[:, :, None],
    ).astype(jnp.bfloat16)
    queries = jnp.concatenate(
        [q_latent.reshape(row_count, step_count, heads_dev, LAT), roped], -1
    ).swapaxes(1, 2)
    queries = queries.reshape(row_count, heads_dev * step_count, channels)
    second = jnp.concatenate([seg_owner, lengths[:, None] // 64, lengths[:, None] % 64], 1)
    second = jnp.pad(second, ((0, 0), (0, 64 - second.shape[1])))
    info = jnp.stack([block_slots, second], 1).astype(jnp.bfloat16)
    info = jnp.pad(info, ((0, 0), (0, heads_dev * step_count - 2), (0, 0)))
    message = jnp.concatenate([queries, info], -1)
    all_queries = lax.all_gather(
        message,
        "cache",
        axis=0,
        tiled=True,
        axis_index_groups=[[y * GROUP + i for i in range(GROUP)] for y in range(NY)],
    )

    nothing = jnp.minimum(lengths[0], 0).astype(hidden.dtype)
    partial_sum = jnp.einsum("rsd,dc->rsc", hidden + nothing, w_dkv, preferred_element_type=jnp.float32)
    summed = lax.psum(partial_sum, "tensor")
    m_a = along_y(half_a, 1)
    p_b = along_y(half_b, -1)
    half_a, half_b, m_a, p_b = gate(half_a, half_b, m_a, p_b)
    m_b = along_y(half_b, 1)
    p_a = along_y(half_a, -1)
    m_l = along_x(m_a, 1)
    p_r = along_x(p_b, -1)
    m_b, p_a, m_l, p_r, m_a, p_b, summed = gate(m_b, p_a, m_l, p_r, m_a, p_b, summed)
    t_a = along_y(m_a, 1)
    t_b = along_y(p_b, -1)
    m_r = along_x(m_b, -1)
    p_l = along_x(p_a, 1)
    new_latent = finish_latent(summed, cosine, sine_part, kv_gain)
    own_scores = (
        jnp.einsum("rqc,rtc->rqt", queries, new_latent, preferred_element_type=jnp.float32)
        * softmax_scale
    )
    steps_of = jnp.arange(heads_dev * step_count) % step_count
    causal = (jnp.arange(step_count)[None, :] <= steps_of[:, None])[None]
    own_masked = jnp.where(causal, own_scores, masked_score)
    own_top = jnp.max(own_masked, -1)
    own_weights = jnp.where(causal, jnp.exp(own_masked - own_top[..., None]), 0.0)
    own_total = jnp.sum(own_weights, -1)
    own_sum = jnp.einsum("rqt,rtl->rql", own_weights, new_latent[..., :LAT].astype(jnp.float32))
    own_b = own_sum.astype(jnp.bfloat16).reshape(row_count, heads_dev, step_count, LAT)
    own_proj = jnp.einsum("rhsl,hlv->rhsv", own_b, w_uv, preferred_element_type=jnp.float32)
    own_proj = own_proj.reshape(row_count, heads_dev * step_count, -1)
    own_part = own_proj / own_total[..., None]
    own_lse = own_top + jnp.log(own_total)

    table = all_queries[:, :2, channels:].astype(jnp.float32).astype(jnp.int32)
    offsets = jnp.array([0, NY - 1, 1, 2], jnp.int32)
    targets = (y_here + offsets) % NY * GROUP + me % GROUP

    def stage_of(name, which, lists, after, earlier=()):
        blocks, live = tables(table, targets[which])
        pieces, arrays = [], []
        for owner, quarters in enumerate(lists):
            if quarters is None:
                pieces.append((owner, "all", 0))
                arrays.append(latent_cache)
            else:
                pieces += [(owner, "mine", 0), (owner, "mine", PAIRS)]
                pieces += [(owner, "other", 0), (owner, "other", PAIRS)]
                arrays += quarters
        return attend(
            all_queries, w_uv, blocks, live, parities, arrays, pieces, len(lists), name, after, earlier
        )

    state = stage_of("first", slice(0, 1), [None], (m_l, p_r))
    t_a, t_b, m_r, p_l, *state = gate(t_a, t_b, m_r, p_l, *state)
    t_l = along_x(t_a, 1)
    t_r = along_x(t_b, -1)
    state = stage_of(
        "middle",
        slice(1, 3),
        [(m_a, m_b, m_l, m_r), (p_a, p_b, p_l, p_r)],
        (t_a, t_b, own_lse),
        tuple(state),
    )
    part, lse = stage_of("last", slice(3, 4), [(t_a, t_b, t_l, t_r)], (), tuple(state))

    width = part.shape[1]
    part = part.reshape(NZ, NC, row_count, width, -1)
    lse = lse[:, :width].reshape(NZ, NC, row_count, width)
    pick = lambda array, which: lax.dynamic_index_in_dim(array, which, 1, keepdims=False)
    mine, theirs = pick(part, core), other_core(pick(part, 1 - core).astype(jnp.bfloat16))
    lse_mine, lse_theirs = pick(lse, core), other_core(pick(lse, 1 - core))
    most = jnp.maximum(lse_mine, lse_theirs)
    w_mine, w_theirs = jnp.exp(lse_mine - most), jnp.exp(lse_theirs - most)
    both = w_mine + w_theirs
    chip_part = mine * (w_mine / both)[..., None] + theirs * (w_theirs / both)[..., None]
    chip_lse = most + jnp.log(both)
    nearest = lambda array: lax.reduce_precision(array, 8, 7)
    high = nearest(chip_lse)
    middle = nearest(chip_lse - high)
    low = chip_lse - high - middle
    stats = jnp.concatenate(
        [jnp.concatenate([high, middle], 2), jnp.concatenate([low, jnp.zeros_like(low)], 2)], 1
    ).astype(jnp.bfloat16)
    chip_part = chip_part.astype(jnp.bfloat16).reshape(NZ, row_count * width, -1)
    along_z = [[place(y, z, c) for z in range(NZ)] for y in range(NY) for c in range(NC)]
    got = lax.all_to_all(
        jnp.concatenate([chip_part, stats], 1),
        "cache",
        split_axis=0,
        concat_axis=0,
        axis_index_groups=along_z,
        tiled=True,
    )
    home_part = got[:, : row_count * width].reshape(NZ, row_count, width, -1)
    stats = got[:, row_count * width :].astype(jnp.float32)
    home_lse = (
        stats[:, :row_count, :width] + stats[:, :row_count, width:]
    ) + stats[:, row_count:, :width]
    largest = jnp.maximum(own_lse, jnp.max(home_lse, 0))
    factor = jnp.exp(home_lse - largest[None])
    own_factor = jnp.exp(own_lse - largest)
    numerator = jnp.sum(factor[..., None] * home_part, 0) + own_factor[..., None] * own_part
    denominator = jnp.sum(factor, 0) + own_factor
    attn_out = (numerator / denominator[..., None]).astype(jnp.bfloat16)
    attn_out = attn_out.reshape(row_count, heads_dev, step_count, -1).swapaxes(1, 2)
    return (attn_out.reshape(row_count, step_count, -1), new_latent)


def solution(mesh):
    in_specs = (
        P("cache", None, "tensor"),
        P("tensor", None),
        P(),
        P("cache", None, "tensor"),
        P("cache", None, "tensor"),
        P("tensor", None, None),
        P("cache", None, None),
        P("cache", None),
        P("cache", None),
        P("cache"),
    )
    out_specs = (P("cache", None, "tensor"), P("cache", None, None))
    return jax.shard_map(body, mesh=mesh, in_specs=in_specs, out_specs=out_specs, check_vma=False)
```

```python
import functools

import jax
import jax.numpy as jnp
from jax import lax
from jax.experimental import pallas as pl
from jax.experimental.pallas import tpu as pltpu
from jax.sharding import PartitionSpec as P

LAT = 512
SEGS = 8
NY, NZ, NC, NX = 4, 8, 2, 4
GROUP = NZ * NC
WIDE = 640
AT_ONCE = 4
PAIRS = 8
VMEM_BYTES = 60 * 1024 * 1024

softmax_scale = 192.0 ** (-0.5)
masked_score = -1e30
rope_base = 10000.0


def place(y, z, c):
    return (y % NY * NZ + z % NZ) * NC + c


def spots():
    return [(y, z, c) for y in range(NY) for z in range(NZ) for c in range(NC)]


def along_y(array, by):
    return lax.ppermute(
        array, "cache", [(place(y, z, c), place(y + by, z, c)) for y, z, c in spots()]
    )


def along_x(array, by):
    return lax.ppermute(array, "tensor", [(i, (i + by) % NX) for i in range(NX)])


def other_core(array):
    return lax.ppermute(
        array, "cache", [(place(y, z, c), place(y, z, 1 - c)) for y, z, c in spots()]
    )


def angle_tables(places, width):
    half_width = width // 2
    frequency = rope_base ** (-(jnp.arange(half_width, dtype=jnp.float32) * 2.0 / width))
    angles = places.astype(jnp.float32)[..., None] * frequency
    return lax.optimization_barrier((jnp.cos(angles), jnp.sin(angles)))


def rotate(values, cosine, sine_part):
    half_width = values.shape[-1] // 2
    front_half = values[..., :half_width]
    back_half = values[..., half_width:]
    return jnp.concatenate(
        [front_half * cosine - back_half * sine_part, front_half * sine_part + back_half * cosine],
        -1,
    )


def finish_latent(summed, cosine, sine_part, kv_gain):
    latent = summed[..., :LAT]
    normed = latent * lax.rsqrt(jnp.mean(latent * latent, -1, keepdims=True) + 1e-06) * kv_gain
    roped = rotate(summed[..., LAT:], cosine, sine_part)
    return jnp.concatenate([normed, roped], -1).astype(jnp.bfloat16)


def gate(*arrays):
    anywhere = pl.BlockSpec(memory_space=pltpu.HBM)
    return pl.pallas_call(
        lambda *refs: None,
        out_shape=[jax.ShapeDtypeStruct(a.shape, a.dtype) for a in arrays],
        in_specs=[anywhere] * len(arrays),
        out_specs=[anywhere] * len(arrays),
        input_output_aliases={i: i for i in range(len(arrays))},
        compiler_params=pltpu.CompilerParams(vmem_limit_bytes=VMEM_BYTES),
    )(*arrays)


def pack_kernel(par_ref, len_in, cache, out_a, out_b, len_out, held, packed, in_sems, out_sems):
    count = 4
    blocks, pairs = 32 // count, 2 * PAIRS // count
    first = par_ref[0] * 32
    copies = [
        pltpu.make_async_copy(
            cache.at[pl.ds(first + n * blocks, blocks)],
            held.at[pl.ds(n * blocks, blocks)],
            in_sems.at[n],
        )
        for n in range(count)
    ]
    for copy in copies:
        copy.start()
    for row in range(len_in.shape[0]):
        len_out[row] = len_in[row]
    sends = []
    for n in range(count):
        copies[n].wait()

        def one(pair, carry):
            ropes = []
            for b in range(2):
                block = held[2 * pair + b]
                packed[pair, 64 * b : 64 * b + 64, :] = block[:, :LAT]
                rope = block[:, LAT:]
                rope = jnp.concatenate([rope[:32], rope[32:]], 1)
                ropes += [rope[:16], rope[16:]]
            packed[pair, 128:, :] = jnp.concatenate(ropes, 1)
            return carry

        lax.fori_loop(n * pairs, (n + 1) * pairs, one, 0)
        out = out_a if n < count // 2 else out_b
        sends.append(
            pltpu.make_async_copy(
                packed.at[pl.ds(n * pairs, pairs)],
                out.at[pl.ds(n * pairs % PAIRS, pairs)],
                out_sems.at[n],
            )
        )
        sends[-1].start()
    for send in sends:
        send.wait()


def pack(latent_cache, parity, lengths):
    shape = jax.ShapeDtypeStruct((PAIRS, 144, LAT), latent_cache.dtype)
    return pl.pallas_call(
        pack_kernel,
        out_shape=[shape, shape, jax.ShapeDtypeStruct(lengths.shape, lengths.dtype)],
        grid_spec=pltpu.PrefetchScalarGridSpec(
            num_scalar_prefetch=2,
            grid=(),
            in_specs=[pl.BlockSpec(memory_space=pltpu.HBM)],
            out_specs=[pl.BlockSpec(memory_space=pltpu.HBM)] * 2
            + [pl.BlockSpec(memory_space=pltpu.SMEM)],
            scratch_shapes=[
                pltpu.VMEM((32,) + latent_cache.shape[1:], latent_cache.dtype),
                pltpu.VMEM((2 * PAIRS,) + shape.shape[1:], latent_cache.dtype),
                pltpu.SemaphoreType.DMA((4,)),
                pltpu.SemaphoreType.DMA((4,)),
            ],
        ),
        compiler_params=pltpu.CompilerParams(vmem_limit_bytes=VMEM_BYTES),
    )(parity, lengths, latent_cache)


def attend_kernel(owners, pieces, unused, stage, *refs):
    blk_ref, live_ref, par_ref, q_in, w_in = refs[:5]
    refs = refs[5:]
    kv_in = refs[: len(pieces)]
    refs = refs[len(pieces) + unused :]
    if stage != "first":
        state_in, lse_in = refs[:2]
        refs = refs[2:]
    state, lse_ref, kv, queries, normal, slot_lse, projected, w_ref, items, kv_sems, q_sems, row_sems = refs
    rows = lse_ref.shape[0]

    copies = [[] for _ in range(owners)]
    for n, (owner, side, offset) in enumerate(pieces):
        first = owner * 4 * PAIRS + offset
        if side == "mine":
            first = first + par_ref[0] * 2 * PAIRS
        elif side == "other":
            first = first + (1 - par_ref[0]) * 2 * PAIRS
        copies[owner].append(
            pltpu.make_async_copy(
                kv_in[n], kv.at[pl.ds(first, kv_in[n].shape[0])], kv_sems.at[n]
            )
        )
    for some in copies:
        for copy in some:
            copy.start()
    extra = [pltpu.make_async_copy(w_in, w_ref, kv_sems.at[len(pieces)])]
    if stage != "first":
        extra.append(pltpu.make_async_copy(lse_in, lse_ref, kv_sems.at[len(pieces) + 1]))
    if stage == "middle":
        extra.append(pltpu.make_async_copy(state_in, state, kv_sems.at[len(pieces) + 2]))

    def scan(i, n):
        items[n] = i
        return n + (live_ref[i] > 0).astype(jnp.int32)

    ends = [jnp.int32(0)]
    for o in range(owners):
        ends.append(lax.fori_loop(o * rows, (o + 1) * rows, scan, ends[-1], unroll=8))
    found = ends[-1]

    def row_of(slot):
        return items[slot] & (rows - 1)

    def fetch(slot):
        return pltpu.make_async_copy(q_in.at[row_of(slot)], queries.at[slot], q_sems.at[slot])

    def load_row(slot):
        return pltpu.make_async_copy(state.at[row_of(slot)], normal.at[slot, :, :128], row_sems.at[slot])

    def store_row(slot):
        return pltpu.make_async_copy(projected.at[slot], state.at[row_of(slot)], row_sems.at[slot])

    def each(action):
        def step(slot, carry):
            action(slot)
            return carry

        lax.fori_loop(0, found, step, 0)

    each(lambda slot: fetch(slot).start())
    if stage == "first":
        state[...] = jnp.zeros_like(state)
        lse_ref[...] = jnp.full_like(lse_ref, masked_score)

    low_lanes = lax.broadcasted_iota(jnp.int32, (16, 128), 1) < 64

    def blocks_of(slot):
        item = items[slot]
        return [(item // rows) * 64 + blk_ref[item * 8 + t] for t in range(8)]

    def latents(b):
        if stage == "first":
            return kv[b, :, :LAT]
        return kv[b // 2, pl.ds(pl.multiple_of((b & 1) * 64, 64), 64), :]

    def keys(b):
        if stage == "first":
            return kv[b]
        some = kv[b // 2, 128:, pl.ds(pl.multiple_of((b & 1) * 256, 256), 256)]
        nothing = jnp.zeros((16, 128), some.dtype)
        groups = [some[:, :128], some[:, 128:]]
        ropes = [jnp.where(low_lanes, g, nothing) for g in groups]
        ropes += [jnp.where(low_lanes, nothing, g) for g in groups]
        return jnp.concatenate([latents(b), jnp.concatenate(ropes, 0)], 1)

    def score_of(slot, blocks):
        q = queries[slot]
        channels = LAT + 64
        q = q[:, :channels]
        if stage != "first":
            q = jnp.concatenate([q, q[:, LAT:]], 1)
        scores = []
        for h in range(2):
            some = jnp.concatenate([keys(b) for b in blocks[4 * h : 4 * h + 4]], 0)
            scores.append(
                lax.dot_general(
                    q, some, (((1,), (1,)), ((), ())), preferred_element_type=jnp.float32
                )
            )
        return jnp.concatenate(scores, 1) * softmax_scale

    def soften(score, live):
        alive = lax.broadcasted_iota(jnp.int32, score.shape, 1) < live
        masked = jnp.where(alive, score, masked_score)
        highest = jnp.max(masked, 1, keepdims=True)
        weights = jnp.where(alive, jnp.exp(masked - highest), 0.0)
        summed = jnp.sum(weights, 1, keepdims=True)
        return weights.astype(jnp.bfloat16), 1.0 / summed, highest + jnp.log(summed)

    def value_of(weights_b, blocks):
        result = None
        for h in range(2):
            vals = jnp.concatenate([latents(b) for b in blocks[4 * h : 4 * h + 4]], 0)
            part = jnp.dot(
                weights_b[:, 256 * h : 256 * h + 256], vals, preferred_element_type=jnp.float32
            )
            result = part if result is None else result + part
        return result

    for o in range(owners):
        begin, end = ends[o], ends[o + 1]
        for copy in copies[o]:
            copy.wait()
        if o == 0:
            for copy in extra:
                copy.start()

        def several(j, carry):
            first = begin + AT_ONCE * j
            group = [jnp.minimum(first + i, end - 1) for i in range(AT_ONCE)]
            for i, slot in enumerate(group):

                @pl.when(first + i < end)
                def _():
                    fetch(slot).wait()

            blocks = [blocks_of(slot) for slot in group]
            scores = [score_of(slot, some) for slot, some in zip(group, blocks)]
            soft = [soften(score, live_ref[items[slot]]) for score, slot in zip(scores, group)]
            results = [value_of(one[0], some) for one, some in zip(soft, blocks)]
            for slot, one, result in zip(group, soft, results):
                normal[slot] = result * one[1]
                slot_lse[slot] = jnp.broadcast_to(one[2], slot_lse.shape[1:])
            return carry

        lax.fori_loop(0, (end - begin + AT_ONCE - 1) // AT_ONCE, several, 0)

    for copy in extra:
        copy.wait()

    def project(group, carry):
        some = pl.ds(pl.multiple_of(group * 32, 32), 32)
        for j in range(8):
            span = slice(8 * j, 8 * j + 8)
            x = normal[some, span, :].reshape(32 * 8, LAT).astype(jnp.bfloat16)
            w = jnp.concatenate([w_ref[2 * j], w_ref[2 * j + 1]], 1)
            y = jnp.dot(x, w, preferred_element_type=jnp.float32)
            upper = (lax.broadcasted_iota(jnp.int32, (32 * 8, 128), 0) & 7) < 4
            projected[some, span, :] = jnp.where(upper, y[:, :128], y[:, 128:]).reshape(32, 8, 128)
        return carry

    lax.fori_loop(0, (found + 31) // 32, project, 0)
    if stage == "last":
        each(lambda slot: load_row(slot).start())
        each(lambda slot: load_row(slot).wait())

    diagonal = lax.broadcasted_iota(jnp.int32, (64, 128), 0) == lax.broadcasted_iota(
        jnp.int32, (64, 128), 1
    )
    for o in range(owners):
        begin, end = ends[o], ends[o + 1]

        def merge(j, carry):
            group = [jnp.minimum(begin + AT_ONCE * j + i, end - 1) for i in range(AT_ONCE)]
            where = [row_of(slot) for slot in group]
            values = []
            for slot, row in zip(group, where):
                across = jnp.broadcast_to(lse_ref[pl.ds(row, 1), :], (64, 128))
                before = jnp.sum(jnp.where(diagonal, across, 0.0), 1, keepdims=True)
                added = slot_lse[slot]
                most = jnp.maximum(before, added)
                keep = jnp.exp(before - most)
                add = jnp.exp(added - most)
                both = keep + add
                lse = most + jnp.log(both)
                lse_row = jnp.sum(jnp.where(diagonal, lse, 0.0), 0, keepdims=True)
                old = normal[slot, :, :128] if stage == "last" else state[row]
                values.append((lse_row, (old * keep + projected[slot] * add) / both))
            for slot, row, (lse_row, value) in zip(group, where, values):
                lse_ref[pl.ds(row, 1), :] = lse_row
                if stage == "last":
                    projected[slot] = value
                else:
                    state[row] = value
            return carry

        lax.fori_loop(0, (end - begin + AT_ONCE - 1) // AT_ONCE, merge, 0)
    if stage == "last":
        each(lambda slot: store_row(slot).start())
        each(lambda slot: store_row(slot).wait())


def attend(queries, w_uv, blocks, live, parity, arrays, pieces, owners, stage, after, earlier):
    rows = queries.shape[0]
    slots = owners * GROUP * 2
    all_blocks = (owners * 64,) if stage == "first" else (owners * 4 * PAIRS,)
    whole = pl.BlockSpec(memory_space=pltpu.VMEM)
    anywhere = pl.BlockSpec(memory_space=pltpu.HBM)
    in_specs = [anywhere, anywhere] + [anywhere] * len(arrays)
    in_specs += [anywhere] * len(after)
    operands = [queries, w_uv, *arrays, *after, *earlier]
    if earlier:
        in_specs += [anywhere, anywhere]
    return pl.pallas_call(
        functools.partial(attend_kernel, owners, pieces, len(after), stage),
        out_shape=[
            jax.ShapeDtypeStruct((rows, 64, 128), jnp.float32),
            jax.ShapeDtypeStruct((rows, 128), jnp.float32),
        ],
        grid_spec=pltpu.PrefetchScalarGridSpec(
            num_scalar_prefetch=3,
            grid=(),
            in_specs=in_specs,
            out_specs=[anywhere if stage == "last" else whole, whole],
            scratch_shapes=[
                pltpu.VMEM(all_blocks + arrays[0].shape[1:], jnp.bfloat16),
                pltpu.VMEM((slots, 64, WIDE), jnp.bfloat16),
                pltpu.VMEM((slots, 64, LAT), jnp.float32),
                pltpu.VMEM((slots, 64, 128), jnp.float32),
                pltpu.VMEM((slots, 64, 128), jnp.float32),
                pltpu.VMEM(w_uv.shape, w_uv.dtype),
                pltpu.SMEM((owners * rows,), jnp.int32),
                pltpu.SemaphoreType.DMA((len(arrays) + 3,)),
                pltpu.SemaphoreType.DMA((slots,)),
                pltpu.SemaphoreType.DMA((slots,)),
            ],
        ),
        input_output_aliases={3 + len(operands) - 2: 0} if stage == "last" else {},
        compiler_params=pltpu.CompilerParams(vmem_limit_bytes=VMEM_BYTES),
        cost_estimate=pl.CostEstimate(
            flops=owners * 32 * 64 * 512 * 1088 * 2,
            bytes_accessed=owners * 5 * 2**20 + 2**24,
            transcendentals=owners * 32 * 64 * 512,
        ),
    )(blocks, live, parity, *operands)


def tables(info, targets):
    slots = info[:, 0, :]
    owners = info[:, 1, :SEGS]
    lengths = info[:, 1, SEGS] * 64 + info[:, 1, SEGS + 1]
    rows = info.shape[0]
    segment = jnp.arange(SEGS, dtype=jnp.int32)
    match = (owners[None] == targets[:, None, None]).astype(jnp.int32)
    tokens = jnp.clip(lengths[:, None] - segment[None, :] * 512, 0, 512)
    live = jnp.sum(match * tokens[None], -1)
    blocks = jnp.sum(match[..., None] * slots.reshape(rows, SEGS, SEGS)[None], 2)
    return blocks.reshape(-1), live.reshape(-1)


def body(
    hidden, w_dkv, kv_gain, q_latent, q_rope, w_uv, latent_cache, block_slots, seg_owner, lengths
):
    row_count, step_count = hidden.shape[:2]
    channels = latent_cache.shape[-1]
    heads_dev = q_latent.shape[2] // LAT
    rope_width = channels - LAT
    me = lax.axis_index("cache")
    core = me % NC
    y_here = me // GROUP
    parity = lax.axis_index("tensor") % 2
    parities = parity.astype(jnp.int32)[None]
    half_a, half_b, lengths = pack(latent_cache, parities, lengths)
    positions = lengths[:, None] + jnp.arange(step_count, dtype=jnp.int32)[None, :]

    cosine, sine_part = angle_tables(positions, rope_width)

    roped = rotate(
        q_rope.reshape(row_count, step_count, heads_dev, rope_width).astype(jnp.float32),
        cosine[:, :, None],
        sine_part[:, :, None],
    ).astype(jnp.bfloat16)
    queries = jnp.concatenate(
        [q_latent.reshape(row_count, step_count, heads_dev, LAT), roped], -1
    ).swapaxes(1, 2)
    queries = queries.reshape(row_count, heads_dev * step_count, channels)
    second = jnp.concatenate([seg_owner, lengths[:, None] // 64, lengths[:, None] % 64], 1)
    second = jnp.pad(second, ((0, 0), (0, 64 - second.shape[1])))
    info = jnp.stack([block_slots, second], 1).astype(jnp.bfloat16)
    info = jnp.pad(info, ((0, 0), (0, heads_dev * step_count - 2), (0, 0)))
    message = jnp.concatenate([queries, info], -1)
    all_queries = lax.all_gather(
        message,
        "cache",
        axis=0,
        tiled=True,
        axis_index_groups=[[y * GROUP + i for i in range(GROUP)] for y in range(NY)],
    )

    nothing = jnp.minimum(lengths[0], 0).astype(hidden.dtype)
    partial_sum = jnp.einsum("rsd,dc->rsc", hidden + nothing, w_dkv, preferred_element_type=jnp.float32)
    summed = lax.psum(partial_sum, "tensor")
    m_a = along_y(half_a, 1)
    p_b = along_y(half_b, -1)
    half_a, half_b, m_a, p_b = gate(half_a, half_b, m_a, p_b)
    m_b = along_y(half_b, 1)
    p_a = along_y(half_a, -1)
    m_l = along_x(m_a, 1)
    p_r = along_x(p_b, -1)
    m_b, p_a, m_l, p_r, m_a, p_b, summed = gate(m_b, p_a, m_l, p_r, m_a, p_b, summed)
    t_a = along_y(m_a, 1)
    t_b = along_y(p_b, -1)
    m_r = along_x(m_b, -1)
    p_l = along_x(p_a, 1)
    new_latent = finish_latent(summed, cosine, sine_part, kv_gain)
    own_scores = (
        jnp.einsum("rqc,rtc->rqt", queries, new_latent, preferred_element_type=jnp.float32)
        * softmax_scale
    )
    steps_of = jnp.arange(heads_dev * step_count) % step_count
    causal = (jnp.arange(step_count)[None, :] <= steps_of[:, None])[None]
    own_masked = jnp.where(causal, own_scores, masked_score)
    own_top = jnp.max(own_masked, -1)
    own_weights = jnp.where(causal, jnp.exp(own_masked - own_top[..., None]), 0.0)
    own_total = jnp.sum(own_weights, -1)
    own_sum = jnp.einsum("rqt,rtl->rql", own_weights, new_latent[..., :LAT].astype(jnp.float32))
    own_b = own_sum.astype(jnp.bfloat16).reshape(row_count, heads_dev, step_count, LAT)
    own_proj = jnp.einsum("rhsl,hlv->rhsv", own_b, w_uv, preferred_element_type=jnp.float32)
    own_proj = own_proj.reshape(row_count, heads_dev * step_count, -1)
    own_part = own_proj / own_total[..., None]
    own_lse = own_top + jnp.log(own_total)

    table = all_queries[:, :2, channels:].astype(jnp.float32).astype(jnp.int32)
    offsets = jnp.array([0, NY - 1, 1, 2], jnp.int32)
    targets = (y_here + offsets) % NY * GROUP + me % GROUP

    def stage_of(name, which, lists, after, earlier=()):
        blocks, live = tables(table, targets[which])
        pieces, arrays = [], []
        for owner, quarters in enumerate(lists):
            if quarters is None:
                pieces.append((owner, "all", 0))
                arrays.append(latent_cache)
            else:
                pieces += [(owner, "mine", 0), (owner, "mine", PAIRS)]
                pieces += [(owner, "other", 0), (owner, "other", PAIRS)]
                arrays += quarters
        return attend(
            all_queries, w_uv, blocks, live, parities, arrays, pieces, len(lists), name, after, earlier
        )

    state = stage_of("first", slice(0, 1), [None], (m_l, p_r))
    t_a, t_b, m_r, p_l, *state = gate(t_a, t_b, m_r, p_l, *state)
    t_l = along_x(t_a, 1)
    t_r = along_x(t_b, -1)
    state = stage_of(
        "middle",
        slice(1, 3),
        [(m_a, m_b, m_l, m_r), (p_a, p_b, p_l, p_r)],
        (t_a, t_b, own_lse),
        tuple(state),
    )
    part, lse = stage_of("last", slice(3, 4), [(t_a, t_b, t_l, t_r)], (), tuple(state))

    width = part.shape[1]
    part = part.reshape(NZ, NC, row_count, width, -1)
    lse = lse[:, :width].reshape(NZ, NC, row_count, width)
    pick = lambda array, which: lax.dynamic_index_in_dim(array, which, 1, keepdims=False)
    mine, theirs = pick(part, core), other_core(pick(part, 1 - core).astype(jnp.bfloat16))
    lse_mine, lse_theirs = pick(lse, core), other_core(pick(lse, 1 - core))
    most = jnp.maximum(lse_mine, lse_theirs)
    w_mine, w_theirs = jnp.exp(lse_mine - most), jnp.exp(lse_theirs - most)
    both = w_mine + w_theirs
    chip_part = mine * (w_mine / both)[..., None] + theirs * (w_theirs / both)[..., None]
    chip_lse = most + jnp.log(both)
    nearest = lambda array: lax.reduce_precision(array, 8, 7)
    high = nearest(chip_lse)
    middle = nearest(chip_lse - high)
    low = chip_lse - high - middle
    stats = jnp.concatenate(
        [jnp.concatenate([high, middle], 2), jnp.concatenate([low, jnp.zeros_like(low)], 2)], 1
    ).astype(jnp.bfloat16)
    chip_part = chip_part.astype(jnp.bfloat16).reshape(NZ, row_count * width, -1)
    along_z = [[place(y, z, c) for z in range(NZ)] for y in range(NY) for c in range(NC)]
    got = lax.all_to_all(
        jnp.concatenate([chip_part, stats], 1),
        "cache",
        split_axis=0,
        concat_axis=0,
        axis_index_groups=along_z,
        tiled=True,
    )
    home_part = got[:, : row_count * width].reshape(NZ, row_count, width, -1)
    stats = got[:, row_count * width :].astype(jnp.float32)
    home_lse = (
        stats[:, :row_count, :width] + stats[:, :row_count, width:]
    ) + stats[:, row_count:, :width]
    largest = jnp.maximum(own_lse, jnp.max(home_lse, 0))
    factor = jnp.exp(home_lse - largest[None])
    own_factor = jnp.exp(own_lse - largest)
    numerator = jnp.sum(factor[..., None] * home_part, 0) + own_factor[..., None] * own_part
    denominator = jnp.sum(factor, 0) + own_factor
    attn_out = (numerator / denominator[..., None]).astype(jnp.bfloat16)
    attn_out = attn_out.reshape(row_count, heads_dev, step_count, -1).swapaxes(1, 2)
    return (attn_out.reshape(row_count, step_count, -1), new_latent)


def solution(mesh):
    in_specs = (
        P("cache", None, "tensor"),
        P("tensor", None),
        P(),
        P("cache", None, "tensor"),
        P("cache", None, "tensor"),
        P("tensor", None, None),
        P("cache", None, None),
        P("cache", None),
        P("cache", None),
        P("cache"),
    )
    out_specs = (P("cache", None, "tensor"), P("cache", None, None))
    return jax.shard_map(body, mesh=mesh, in_specs=in_specs, out_specs=out_specs, check_vma=False)
```

```python
import functools

import jax
import jax.numpy as jnp
from jax import lax
from jax.experimental import pallas as pl
from jax.experimental.pallas import tpu as pltpu
from jax.sharding import PartitionSpec as P

LAT = 512
SEGS = 8
NY, NZ, NC, NX = 4, 8, 2, 4
GROUP = NZ * NC
WIDE = 640
AT_ONCE = 4
PAIRS = 8
VMEM_BYTES = 60 * 1024 * 1024

softmax_scale = 192.0 ** (-0.5)
masked_score = -1e30
rope_base = 10000.0


def place(y, z, c):
    return (y % NY * NZ + z % NZ) * NC + c


def spots():
    return [(y, z, c) for y in range(NY) for z in range(NZ) for c in range(NC)]


def along_y(array, by):
    return lax.ppermute(
        array, "cache", [(place(y, z, c), place(y + by, z, c)) for y, z, c in spots()]
    )


def along_x(array, by):
    return lax.ppermute(array, "tensor", [(i, (i + by) % NX) for i in range(NX)])


def other_core(array):
    return lax.ppermute(
        array, "cache", [(place(y, z, c), place(y, z, 1 - c)) for y, z, c in spots()]
    )


def angle_tables(places, width):
    half_width = width // 2
    frequency = rope_base ** (-(jnp.arange(half_width, dtype=jnp.float32) * 2.0 / width))
    angles = places.astype(jnp.float32)[..., None] * frequency
    return lax.optimization_barrier((jnp.cos(angles), jnp.sin(angles)))


def rotate(values, cosine, sine_part):
    half_width = values.shape[-1] // 2
    front_half = values[..., :half_width]
    back_half = values[..., half_width:]
    return jnp.concatenate(
        [front_half * cosine - back_half * sine_part, front_half * sine_part + back_half * cosine],
        -1,
    )


def finish_latent(summed, cosine, sine_part, kv_gain):
    latent = summed[..., :LAT]
    normed = latent * lax.rsqrt(jnp.mean(latent * latent, -1, keepdims=True) + 1e-06) * kv_gain
    roped = rotate(summed[..., LAT:], cosine, sine_part)
    return jnp.concatenate([normed, roped], -1).astype(jnp.bfloat16)


def gate(*arrays):
    anywhere = pl.BlockSpec(memory_space=pltpu.HBM)
    return pl.pallas_call(
        lambda *refs: None,
        out_shape=[jax.ShapeDtypeStruct(a.shape, a.dtype) for a in arrays],
        in_specs=[anywhere] * len(arrays),
        out_specs=[anywhere] * len(arrays),
        input_output_aliases={i: i for i in range(len(arrays))},
        compiler_params=pltpu.CompilerParams(vmem_limit_bytes=VMEM_BYTES),
    )(*arrays)


def pack_kernel(par_ref, len_in, cache, out_a, out_b, len_out, held, packed, in_sems, out_sems):
    count = 4
    blocks, pairs = 32 // count, 2 * PAIRS // count
    first = par_ref[0] * 32
    copies = [
        pltpu.make_async_copy(
            cache.at[pl.ds(first + n * blocks, blocks)],
            held.at[pl.ds(n * blocks, blocks)],
            in_sems.at[n],
        )
        for n in range(count)
    ]
    for copy in copies:
        copy.start()
    for row in range(len_in.shape[0]):
        len_out[row] = len_in[row]
    sends = []
    for n in range(count):
        copies[n].wait()

        def one(pair, carry):
            ropes = []
            for b in range(2):
                block = held[2 * pair + b]
                packed[pair, 64 * b : 64 * b + 64, :] = block[:, :LAT]
                rope = block[:, LAT:]
                rope = jnp.concatenate([rope[:32], rope[32:]], 1)
                ropes += [rope[:16], rope[16:]]
            packed[pair, 128:, :] = jnp.concatenate(ropes, 1)
            return carry

        lax.fori_loop(n * pairs, (n + 1) * pairs, one, 0)
        out = out_a if n < count // 2 else out_b
        sends.append(
            pltpu.make_async_copy(
                packed.at[pl.ds(n * pairs, pairs)],
                out.at[pl.ds(n * pairs % PAIRS, pairs)],
                out_sems.at[n],
            )
        )
        sends[-1].start()
    for send in sends:
        send.wait()


def pack(latent_cache, parity, lengths):
    shape = jax.ShapeDtypeStruct((PAIRS, 144, LAT), latent_cache.dtype)
    return pl.pallas_call(
        pack_kernel,
        out_shape=[shape, shape, jax.ShapeDtypeStruct(lengths.shape, lengths.dtype)],
        grid_spec=pltpu.PrefetchScalarGridSpec(
            num_scalar_prefetch=2,
            grid=(),
            in_specs=[pl.BlockSpec(memory_space=pltpu.HBM)],
            out_specs=[pl.BlockSpec(memory_space=pltpu.HBM)] * 2
            + [pl.BlockSpec(memory_space=pltpu.SMEM)],
            scratch_shapes=[
                pltpu.VMEM((32,) + latent_cache.shape[1:], latent_cache.dtype),
                pltpu.VMEM((2 * PAIRS,) + shape.shape[1:], latent_cache.dtype),
                pltpu.SemaphoreType.DMA((4,)),
                pltpu.SemaphoreType.DMA((4,)),
            ],
        ),
        compiler_params=pltpu.CompilerParams(vmem_limit_bytes=VMEM_BYTES),
    )(parity, lengths, latent_cache)


def attend_kernel(base, owners, pieces, unused, stage, *refs):
    blk_ref, live_ref, par_ref, q_in, w_in = refs[:5]
    refs = refs[5:]
    kv_in = refs[: len(pieces)]
    refs = refs[len(pieces) + unused :]
    if stage != "first":
        state_in, lse_in = refs[:2]
        refs = refs[2:]
    state, lse_ref, kv, queries, normal, slot_lse, projected, w_ref, items, kv_sems, q_sems, row_sems = refs
    rows = lse_ref.shape[0]

    copies = [[] for _ in range(owners)]
    for n, (owner, side, offset) in enumerate(pieces):
        first = owner * 4 * PAIRS + offset
        if side == "mine":
            first = first + par_ref[0] * 2 * PAIRS
        elif side == "other":
            first = first + (1 - par_ref[0]) * 2 * PAIRS
        copies[owner].append(
            pltpu.make_async_copy(
                kv_in[n], kv.at[pl.ds(first, kv_in[n].shape[0])], kv_sems.at[n]
            )
        )
    for copy in copies[0]:
        copy.start()
    extra = [pltpu.make_async_copy(w_in, w_ref, kv_sems.at[len(pieces)])]
    if stage != "first":
        extra.append(pltpu.make_async_copy(lse_in, lse_ref, kv_sems.at[len(pieces) + 1]))
    if stage == "middle":
        extra.append(pltpu.make_async_copy(state_in, state, kv_sems.at[len(pieces) + 2]))

    def scan(i, n):
        items[n] = i
        return n + (live_ref[i] > 0).astype(jnp.int32)

    ends = [jnp.int32(0)]
    for o in range(owners):
        first = (base + o) * rows
        ends.append(lax.fori_loop(first, first + rows, scan, ends[-1], unroll=8))
    found = ends[-1]

    def row_of(slot):
        return items[slot] & (rows - 1)

    def fetch(slot):
        return pltpu.make_async_copy(q_in.at[row_of(slot)], queries.at[slot], q_sems.at[slot])

    def load_row(slot):
        return pltpu.make_async_copy(state.at[row_of(slot)], normal.at[slot, :, :128], row_sems.at[slot])

    def store_row(slot):
        return pltpu.make_async_copy(projected.at[slot], state.at[row_of(slot)], row_sems.at[slot])

    def each(action):
        def step(slot, carry):
            action(slot)
            return carry

        lax.fori_loop(0, found, step, 0)

    each(lambda slot: fetch(slot).start())
    if stage == "first":
        state[...] = jnp.zeros_like(state)
        lse_ref[...] = jnp.full_like(lse_ref, masked_score)

    low_lanes = lax.broadcasted_iota(jnp.int32, (16, 128), 1) < 64

    def blocks_of(slot):
        item = items[slot]
        return [(item // rows - base) * 64 + blk_ref[item * 8 + t] for t in range(8)]

    def latents(b):
        if stage == "first":
            return kv[b, :, :LAT]
        return kv[b // 2, pl.ds(pl.multiple_of((b & 1) * 64, 64), 64), :]

    def keys(b):
        if stage == "first":
            return kv[b]
        some = kv[b // 2, 128:, pl.ds(pl.multiple_of((b & 1) * 256, 256), 256)]
        nothing = jnp.zeros((16, 128), some.dtype)
        groups = [some[:, :128], some[:, 128:]]
        ropes = [jnp.where(low_lanes, g, nothing) for g in groups]
        ropes += [jnp.where(low_lanes, nothing, g) for g in groups]
        return jnp.concatenate([latents(b), jnp.concatenate(ropes, 0)], 1)

    def score_of(slot, blocks):
        q = queries[slot]
        channels = LAT + 64
        q = q[:, :channels]
        if stage != "first":
            q = jnp.concatenate([q, q[:, LAT:]], 1)
        scores = []
        for h in range(2):
            some = jnp.concatenate([keys(b) for b in blocks[4 * h : 4 * h + 4]], 0)
            scores.append(
                lax.dot_general(
                    q, some, (((1,), (1,)), ((), ())), preferred_element_type=jnp.float32
                )
            )
        return jnp.concatenate(scores, 1) * softmax_scale

    def soften(score, live):
        alive = lax.broadcasted_iota(jnp.int32, score.shape, 1) < live
        masked = jnp.where(alive, score, masked_score)
        highest = jnp.max(masked, 1, keepdims=True)
        weights = jnp.where(alive, jnp.exp(masked - highest), 0.0)
        summed = jnp.sum(weights, 1, keepdims=True)
        return weights.astype(jnp.bfloat16), 1.0 / summed, highest + jnp.log(summed)

    def value_of(weights_b, blocks):
        result = None
        for h in range(2):
            vals = jnp.concatenate([latents(b) for b in blocks[4 * h : 4 * h + 4]], 0)
            part = jnp.dot(
                weights_b[:, 256 * h : 256 * h + 256], vals, preferred_element_type=jnp.float32
            )
            result = part if result is None else result + part
        return result

    for o in range(owners):
        begin, end = ends[o], ends[o + 1]
        for copy in copies[o]:
            copy.wait()
        for copy in (copies[o + 1] if o + 1 < owners else []) + (extra if o == 0 else []):
            copy.start()

        def several(j, carry):
            first = begin + AT_ONCE * j
            group = [jnp.minimum(first + i, end - 1) for i in range(AT_ONCE)]
            for i, slot in enumerate(group):

                @pl.when(first + i < end)
                def _():
                    fetch(slot).wait()

            blocks = [blocks_of(slot) for slot in group]
            scores = [score_of(slot, some) for slot, some in zip(group, blocks)]
            soft = [soften(score, live_ref[items[slot]]) for score, slot in zip(scores, group)]
            results = [value_of(one[0], some) for one, some in zip(soft, blocks)]
            for slot, one, result in zip(group, soft, results):
                normal[slot] = result * one[1]
                slot_lse[slot] = jnp.broadcast_to(one[2], slot_lse.shape[1:])
            return carry

        lax.fori_loop(0, (end - begin + AT_ONCE - 1) // AT_ONCE, several, 0)

    for copy in extra:
        copy.wait()

    def project(group, carry):
        some = pl.ds(pl.multiple_of(group * 32, 32), 32)
        for j in range(8):
            span = slice(8 * j, 8 * j + 8)
            x = normal[some, span, :].reshape(32 * 8, LAT).astype(jnp.bfloat16)
            w = jnp.concatenate([w_ref[2 * j], w_ref[2 * j + 1]], 1)
            y = jnp.dot(x, w, preferred_element_type=jnp.float32)
            upper = (lax.broadcasted_iota(jnp.int32, (32 * 8, 128), 0) & 7) < 4
            projected[some, span, :] = jnp.where(upper, y[:, :128], y[:, 128:]).reshape(32, 8, 128)
        return carry

    lax.fori_loop(0, (found + 31) // 32, project, 0)
    if stage == "last":
        each(lambda slot: load_row(slot).start())
        each(lambda slot: load_row(slot).wait())

    diagonal = lax.broadcasted_iota(jnp.int32, (64, 128), 0) == lax.broadcasted_iota(
        jnp.int32, (64, 128), 1
    )
    for o in range(owners):
        begin, end = ends[o], ends[o + 1]

        def merge(j, carry):
            group = [jnp.minimum(begin + AT_ONCE * j + i, end - 1) for i in range(AT_ONCE)]
            where = [row_of(slot) for slot in group]
            values = []
            for slot, row in zip(group, where):
                across = jnp.broadcast_to(lse_ref[pl.ds(row, 1), :], (64, 128))
                before = jnp.sum(jnp.where(diagonal, across, 0.0), 1, keepdims=True)
                added = slot_lse[slot]
                most = jnp.maximum(before, added)
                keep = jnp.exp(before - most)
                add = jnp.exp(added - most)
                both = keep + add
                lse = most + jnp.log(both)
                lse_row = jnp.sum(jnp.where(diagonal, lse, 0.0), 0, keepdims=True)
                old = normal[slot, :, :128] if stage == "last" else state[row]
                values.append((lse_row, (old * keep + projected[slot] * add) / both))
            for slot, row, (lse_row, value) in zip(group, where, values):
                lse_ref[pl.ds(row, 1), :] = lse_row
                if stage == "last":
                    projected[slot] = value
                else:
                    state[row] = value
            return carry

        lax.fori_loop(0, (end - begin + AT_ONCE - 1) // AT_ONCE, merge, 0)
    if stage == "last":
        each(lambda slot: store_row(slot).start())
        each(lambda slot: store_row(slot).wait())


def attend(queries, w_uv, blocks, live, parity, arrays, pieces, base, owners, stage, after, earlier):
    rows = queries.shape[0]
    slots = owners * GROUP * 2
    all_blocks = (owners * 64,) if stage == "first" else (owners * 4 * PAIRS,)
    whole = pl.BlockSpec(memory_space=pltpu.VMEM)
    anywhere = pl.BlockSpec(memory_space=pltpu.HBM)
    in_specs = [anywhere, anywhere] + [anywhere] * len(arrays)
    in_specs += [anywhere] * len(after)
    operands = [queries, w_uv, *arrays, *after, *earlier]
    if earlier:
        in_specs += [anywhere, anywhere]
    return pl.pallas_call(
        functools.partial(attend_kernel, base, owners, pieces, len(after), stage),
        out_shape=[
            jax.ShapeDtypeStruct((rows, 64, 128), jnp.float32),
            jax.ShapeDtypeStruct((rows, 128), jnp.float32),
        ],
        grid_spec=pltpu.PrefetchScalarGridSpec(
            num_scalar_prefetch=3,
            grid=(),
            in_specs=in_specs,
            out_specs=[anywhere if stage == "last" else whole, whole],
            scratch_shapes=[
                pltpu.VMEM(all_blocks + arrays[0].shape[1:], jnp.bfloat16),
                pltpu.VMEM((slots, 64, WIDE), jnp.bfloat16),
                pltpu.VMEM((slots, 64, LAT), jnp.float32),
                pltpu.VMEM((slots, 64, 128), jnp.float32),
                pltpu.VMEM((slots, 64, 128), jnp.float32),
                pltpu.VMEM(w_uv.shape, w_uv.dtype),
                pltpu.SMEM((owners * rows,), jnp.int32),
                pltpu.SemaphoreType.DMA((len(arrays) + 3,)),
                pltpu.SemaphoreType.DMA((slots,)),
                pltpu.SemaphoreType.DMA((slots,)),
            ],
        ),
        input_output_aliases={3 + len(operands) - 2: 0} if stage == "last" else {},
        compiler_params=pltpu.CompilerParams(vmem_limit_bytes=VMEM_BYTES),
        cost_estimate=pl.CostEstimate(
            flops=owners * 32 * 64 * 512 * 1088 * 2,
            bytes_accessed=owners * 5 * 2**20 + 2**24,
            transcendentals=owners * 32 * 64 * 512,
        ),
    )(blocks, live, parity, *operands)


def tables(info, targets):
    slots = info[:, 0, :]
    owners = info[:, 1, :SEGS]
    lengths = info[:, 1, SEGS] * 64 + info[:, 1, SEGS + 1]
    rows = info.shape[0]
    segment = jnp.arange(SEGS, dtype=jnp.int32)
    match = (owners[None] == targets[:, None, None]).astype(jnp.int32)
    tokens = jnp.clip(lengths[:, None] - segment[None, :] * 512, 0, 512)
    live = jnp.sum(match * tokens[None], -1)
    blocks = jnp.sum(match[..., None] * slots.reshape(rows, SEGS, SEGS)[None], 2)
    return blocks.reshape(-1), live.reshape(-1)


def body(
    hidden, w_dkv, kv_gain, q_latent, q_rope, w_uv, latent_cache, block_slots, seg_owner, lengths
):
    row_count, step_count = hidden.shape[:2]
    channels = latent_cache.shape[-1]
    heads_dev = q_latent.shape[2] // LAT
    rope_width = channels - LAT
    me = lax.axis_index("cache")
    core = me % NC
    y_here = me // GROUP
    parity = lax.axis_index("tensor") % 2
    parities = parity.astype(jnp.int32)[None]
    half_a, half_b, lengths = pack(latent_cache, parities, lengths)
    positions = lengths[:, None] + jnp.arange(step_count, dtype=jnp.int32)[None, :]

    cosine, sine_part = angle_tables(positions, rope_width)

    roped = rotate(
        q_rope.reshape(row_count, step_count, heads_dev, rope_width).astype(jnp.float32),
        cosine[:, :, None],
        sine_part[:, :, None],
    ).astype(jnp.bfloat16)
    queries = jnp.concatenate(
        [q_latent.reshape(row_count, step_count, heads_dev, LAT), roped], -1
    ).swapaxes(1, 2)
    queries = queries.reshape(row_count, heads_dev * step_count, channels)
    second = jnp.concatenate([seg_owner, lengths[:, None] // 64, lengths[:, None] % 64], 1)
    second = jnp.pad(second, ((0, 0), (0, 64 - second.shape[1])))
    info = jnp.stack([block_slots, second], 1).astype(jnp.bfloat16)
    info = jnp.pad(info, ((0, 0), (0, heads_dev * step_count - 2), (0, 0)))
    message = jnp.concatenate([queries, info], -1)
    all_queries = lax.all_gather(
        message,
        "cache",
        axis=0,
        tiled=True,
        axis_index_groups=[[y * GROUP + i for i in range(GROUP)] for y in range(NY)],
    )

    nothing = jnp.minimum(lengths[0], 0).astype(hidden.dtype)
    partial_sum = jnp.einsum("rsd,dc->rsc", hidden + nothing, w_dkv, preferred_element_type=jnp.float32)
    summed = lax.psum(partial_sum, "tensor")
    m_a = along_y(half_a, 1)
    p_b = along_y(half_b, -1)
    half_a, half_b, m_a, p_b = gate(half_a, half_b, m_a, p_b)
    m_b = along_y(half_b, 1)
    p_a = along_y(half_a, -1)
    m_l = along_x(m_a, 1)
    p_r = along_x(p_b, -1)
    m_b, p_a, m_l, p_r, m_a, p_b, summed = gate(m_b, p_a, m_l, p_r, m_a, p_b, summed)
    t_a = along_y(m_a, 1)
    t_b = along_y(p_b, -1)
    m_r = along_x(m_b, -1)
    p_l = along_x(p_a, 1)
    new_latent = finish_latent(summed, cosine, sine_part, kv_gain)
    own_scores = (
        jnp.einsum("rqc,rtc->rqt", queries, new_latent, preferred_element_type=jnp.float32)
        * softmax_scale
    )
    steps_of = jnp.arange(heads_dev * step_count) % step_count
    causal = (jnp.arange(step_count)[None, :] <= steps_of[:, None])[None]
    own_masked = jnp.where(causal, own_scores, masked_score)
    own_top = jnp.max(own_masked, -1)
    own_weights = jnp.where(causal, jnp.exp(own_masked - own_top[..., None]), 0.0)
    own_total = jnp.sum(own_weights, -1)
    own_sum = jnp.einsum("rqt,rtl->rql", own_weights, new_latent[..., :LAT].astype(jnp.float32))
    own_b = own_sum.astype(jnp.bfloat16).reshape(row_count, heads_dev, step_count, LAT)
    own_proj = jnp.einsum("rhsl,hlv->rhsv", own_b, w_uv, preferred_element_type=jnp.float32)
    own_proj = own_proj.reshape(row_count, heads_dev * step_count, -1)
    own_part = own_proj / own_total[..., None]
    own_lse = own_top + jnp.log(own_total)

    table = all_queries[:, :2, channels:].astype(jnp.float32).astype(jnp.int32)
    offsets = jnp.array([0, NY - 1, 1, 2], jnp.int32)
    targets = (y_here + offsets) % NY * GROUP + me % GROUP

    blocks, live = tables(table, targets)

    def stage_of(name, base, lists, after, earlier=()):
        pieces, arrays = [], []
        for owner, quarters in enumerate(lists):
            if quarters is None:
                pieces.append((owner, "all", 0))
                arrays.append(latent_cache)
            else:
                pieces += [(owner, "mine", 0), (owner, "mine", PAIRS)]
                pieces += [(owner, "other", 0), (owner, "other", PAIRS)]
                arrays += quarters
        return attend(
            all_queries,
            w_uv,
            blocks,
            live,
            parities,
            arrays,
            pieces,
            base,
            len(lists),
            name,
            after,
            earlier,
        )

    state = stage_of("first", 0, [None], (m_l, p_r))
    t_a, t_b, m_r, p_l, own_lse, *state = gate(t_a, t_b, m_r, p_l, own_lse, *state)
    t_l = along_x(t_a, 1)
    t_r = along_x(t_b, -1)
    state = stage_of(
        "middle",
        1,
        [(m_a, m_b, m_l, m_r), (p_a, p_b, p_l, p_r)],
        (t_a, t_b),
        tuple(state),
    )
    part, lse = stage_of("last", 3, [(t_a, t_b, t_l, t_r)], (), tuple(state))

    width = part.shape[1]
    part = part.reshape(NZ, NC, row_count, width, -1)
    lse = lse[:, :width].reshape(NZ, NC, row_count, width)
    pick = lambda array, which: lax.dynamic_index_in_dim(array, which, 1, keepdims=False)
    theirs = other_core(pick(part, 1 - core).astype(jnp.bfloat16))
    part, theirs = gate(part, theirs)
    mine = pick(part, core)
    lse_mine, lse_theirs = pick(lse, core), other_core(pick(lse, 1 - core))
    most = jnp.maximum(lse_mine, lse_theirs)
    w_mine, w_theirs = jnp.exp(lse_mine - most), jnp.exp(lse_theirs - most)
    both = w_mine + w_theirs
    chip_part = mine * (w_mine / both)[..., None] + theirs * (w_theirs / both)[..., None]
    chip_lse = most + jnp.log(both)
    nearest = lambda array: lax.reduce_precision(array, 8, 7)
    high = nearest(chip_lse)
    middle = nearest(chip_lse - high)
    low = chip_lse - high - middle
    stats = jnp.concatenate(
        [jnp.concatenate([high, middle], 2), jnp.concatenate([low, jnp.zeros_like(low)], 2)], 1
    ).astype(jnp.bfloat16)
    chip_part = chip_part.astype(jnp.bfloat16).reshape(NZ, row_count * width, -1)
    along_z = [[place(y, z, c) for z in range(NZ)] for y in range(NY) for c in range(NC)]
    got = lax.all_to_all(
        jnp.concatenate([chip_part, stats], 1),
        "cache",
        split_axis=0,
        concat_axis=0,
        axis_index_groups=along_z,
        tiled=True,
    )
    home_part = got[:, : row_count * width].reshape(NZ, row_count, width, -1)
    stats = got[:, row_count * width :].astype(jnp.float32)
    home_lse = (
        stats[:, :row_count, :width] + stats[:, :row_count, width:]
    ) + stats[:, row_count:, :width]
    largest = jnp.maximum(own_lse, jnp.max(home_lse, 0))
    factor = jnp.exp(home_lse - largest[None])
    own_factor = jnp.exp(own_lse - largest)
    numerator = jnp.sum(factor[..., None] * home_part, 0) + own_factor[..., None] * own_part
    denominator = jnp.sum(factor, 0) + own_factor
    attn_out = (numerator / denominator[..., None]).astype(jnp.bfloat16)
    attn_out = attn_out.reshape(row_count, heads_dev, step_count, -1).swapaxes(1, 2)
    return (attn_out.reshape(row_count, step_count, -1), new_latent)


def solution(mesh):
    in_specs = (
        P("cache", None, "tensor"),
        P("tensor", None),
        P(),
        P("cache", None, "tensor"),
        P("cache", None, "tensor"),
        P("tensor", None, None),
        P("cache", None, None),
        P("cache", None),
        P("cache", None),
        P("cache"),
    )
    out_specs = (P("cache", None, "tensor"), P("cache", None, None))
    return jax.shard_map(body, mesh=mesh, in_specs=in_specs, out_specs=out_specs, check_vma=False)
```

```python
import functools

import jax
import jax.numpy as jnp
from jax import lax
from jax.experimental import pallas as pl
from jax.experimental.pallas import tpu as pltpu
from jax.sharding import PartitionSpec as P

LAT = 512
SEGS = 8
NY, NZ, NC, NX = 4, 8, 2, 4
GROUP = NZ * NC
WIDE = 640
AT_ONCE = 4
PAIRS = 8
VMEM_BYTES = 60 * 1024 * 1024

softmax_scale = 192.0 ** (-0.5)
masked_score = -1e30
rope_base = 10000.0


def place(y, z, c):
    return (y % NY * NZ + z % NZ) * NC + c


def spots():
    return [(y, z, c) for y in range(NY) for z in range(NZ) for c in range(NC)]


def along_y(array, by):
    return lax.ppermute(
        array, "cache", [(place(y, z, c), place(y + by, z, c)) for y, z, c in spots()]
    )


def along_x(array, by):
    return lax.ppermute(array, "tensor", [(i, (i + by) % NX) for i in range(NX)])


def other_core(array):
    return lax.ppermute(
        array, "cache", [(place(y, z, c), place(y, z, 1 - c)) for y, z, c in spots()]
    )


def angle_tables(places, width):
    half_width = width // 2
    frequency = rope_base ** (-(jnp.arange(half_width, dtype=jnp.float32) * 2.0 / width))
    angles = places.astype(jnp.float32)[..., None] * frequency
    return lax.optimization_barrier((jnp.cos(angles), jnp.sin(angles)))


def rotate(values, cosine, sine_part):
    half_width = values.shape[-1] // 2
    front_half = values[..., :half_width]
    back_half = values[..., half_width:]
    return jnp.concatenate(
        [front_half * cosine - back_half * sine_part, front_half * sine_part + back_half * cosine],
        -1,
    )


def finish_latent(summed, cosine, sine_part, kv_gain):
    latent = summed[..., :LAT]
    normed = latent * lax.rsqrt(jnp.mean(latent * latent, -1, keepdims=True) + 1e-06) * kv_gain
    roped = rotate(summed[..., LAT:], cosine, sine_part)
    return jnp.concatenate([normed, roped], -1).astype(jnp.bfloat16)


def gate(*arrays):
    anywhere = pl.BlockSpec(memory_space=pltpu.HBM)
    return pl.pallas_call(
        lambda *refs: None,
        out_shape=[jax.ShapeDtypeStruct(a.shape, a.dtype) for a in arrays],
        in_specs=[anywhere] * len(arrays),
        out_specs=[anywhere] * len(arrays),
        input_output_aliases={i: i for i in range(len(arrays))},
        compiler_params=pltpu.CompilerParams(vmem_limit_bytes=VMEM_BYTES),
    )(*arrays)


def pack_kernel(par_ref, len_in, cache, out_a, out_b, len_out, held, packed, in_sems, out_sems):
    count = 4
    blocks, pairs = 32 // count, 2 * PAIRS // count
    first = par_ref[0] * 32
    copies = [
        pltpu.make_async_copy(
            cache.at[pl.ds(first + n * blocks, blocks)],
            held.at[pl.ds(n * blocks, blocks)],
            in_sems.at[n],
        )
        for n in range(count)
    ]
    for copy in copies:
        copy.start()
    for row in range(len_in.shape[0]):
        len_out[row] = len_in[row]
    sends = []
    for n in range(count):
        copies[n].wait()

        def one(pair, carry):
            ropes = []
            for b in range(2):
                block = held[2 * pair + b]
                packed[pair, 64 * b : 64 * b + 64, :] = block[:, :LAT]
                rope = block[:, LAT:]
                rope = jnp.concatenate([rope[:32], rope[32:]], 1)
                ropes += [rope[:16], rope[16:]]
            packed[pair, 128:, :] = jnp.concatenate(ropes, 1)
            return carry

        lax.fori_loop(n * pairs, (n + 1) * pairs, one, 0)
        out = out_a if n < count // 2 else out_b
        sends.append(
            pltpu.make_async_copy(
                packed.at[pl.ds(n * pairs, pairs)],
                out.at[pl.ds(n * pairs % PAIRS, pairs)],
                out_sems.at[n],
            )
        )
        sends[-1].start()
    for send in sends:
        send.wait()


def pack(latent_cache, parity, lengths):
    shape = jax.ShapeDtypeStruct((PAIRS, 144, LAT), latent_cache.dtype)
    return pl.pallas_call(
        pack_kernel,
        out_shape=[shape, shape, jax.ShapeDtypeStruct(lengths.shape, lengths.dtype)],
        grid_spec=pltpu.PrefetchScalarGridSpec(
            num_scalar_prefetch=2,
            grid=(),
            in_specs=[pl.BlockSpec(memory_space=pltpu.HBM)],
            out_specs=[pl.BlockSpec(memory_space=pltpu.HBM)] * 2
            + [pl.BlockSpec(memory_space=pltpu.SMEM)],
            scratch_shapes=[
                pltpu.VMEM((32,) + latent_cache.shape[1:], latent_cache.dtype),
                pltpu.VMEM((2 * PAIRS,) + shape.shape[1:], latent_cache.dtype),
                pltpu.SemaphoreType.DMA((4,)),
                pltpu.SemaphoreType.DMA((4,)),
            ],
        ),
        compiler_params=pltpu.CompilerParams(vmem_limit_bytes=VMEM_BYTES),
    )(parity, lengths, latent_cache)


def attend_kernel(base, owners, pieces, unused, stage, *refs):
    blk_ref, live_ref, par_ref, q_in, w_in = refs[:5]
    refs = refs[5:]
    kv_in = refs[: len(pieces)]
    refs = refs[len(pieces) + unused :]
    if stage != "first":
        state_in, lse_in = refs[:2]
        refs = refs[2:]
    state, lse_ref, kv, queries, normal, slot_lse, projected, w_ref, items, kv_sems, q_sems, row_sems = refs
    rows = lse_ref.shape[0]

    copies = [[] for _ in range(owners)]
    for n, (owner, side, offset) in enumerate(pieces):
        first = owner * 4 * PAIRS + offset
        if side == "mine":
            first = first + par_ref[0] * 2 * PAIRS
        elif side == "other":
            first = first + (1 - par_ref[0]) * 2 * PAIRS
        copies[owner].append(
            pltpu.make_async_copy(
                kv_in[n], kv.at[pl.ds(first, kv_in[n].shape[0])], kv_sems.at[n]
            )
        )
    for copy in copies[0]:
        copy.start()
    extra = [pltpu.make_async_copy(w_in, w_ref, kv_sems.at[len(pieces)])]
    if stage != "first":
        extra.append(pltpu.make_async_copy(lse_in, lse_ref, kv_sems.at[len(pieces) + 1]))
    if stage == "middle":
        extra.append(pltpu.make_async_copy(state_in, state, kv_sems.at[len(pieces) + 2]))

    def scan(i, n):
        items[n] = i
        return n + (live_ref[i] > 0).astype(jnp.int32)

    ends = [jnp.int32(0)]
    for o in range(owners):
        first = (base + o) * rows
        ends.append(lax.fori_loop(first, first + rows, scan, ends[-1], unroll=8))
    found = ends[-1]

    def row_of(slot):
        return items[slot] & (rows - 1)

    def fetch(slot):
        return pltpu.make_async_copy(q_in.at[row_of(slot)], queries.at[slot], q_sems.at[slot])

    def load_row(slot):
        return pltpu.make_async_copy(state.at[row_of(slot)], normal.at[slot, :, :128], row_sems.at[slot])

    def store_row(slot):
        return pltpu.make_async_copy(projected.at[slot], state.at[row_of(slot)], row_sems.at[slot])

    def each(action):
        def step(slot, carry):
            action(slot)
            return carry

        lax.fori_loop(0, found, step, 0)

    each(lambda slot: fetch(slot).start())
    if stage == "first":
        state[...] = jnp.zeros_like(state)
        lse_ref[...] = jnp.full_like(lse_ref, masked_score)

    low_lanes = lax.broadcasted_iota(jnp.int32, (16, 128), 1) < 64

    def blocks_of(slot):
        item = items[slot]
        return [(item // rows - base) * 64 + blk_ref[item * 8 + t] for t in range(8)]

    def latents(b):
        if stage == "first":
            return kv[b, :, :LAT]
        return kv[b // 2, pl.ds(pl.multiple_of((b & 1) * 64, 64), 64), :]

    def keys(b):
        if stage == "first":
            return kv[b]
        some = kv[b // 2, 128:, pl.ds(pl.multiple_of((b & 1) * 256, 256), 256)]
        nothing = jnp.zeros((16, 128), some.dtype)
        groups = [some[:, :128], some[:, 128:]]
        ropes = [jnp.where(low_lanes, g, nothing) for g in groups]
        ropes += [jnp.where(low_lanes, nothing, g) for g in groups]
        return jnp.concatenate([latents(b), jnp.concatenate(ropes, 0)], 1)

    def score_of(slot, blocks):
        q = queries[slot]
        channels = LAT + 64
        q = q[:, :channels]
        if stage != "first":
            q = jnp.concatenate([q, q[:, LAT:]], 1)
        scores = []
        for h in range(2):
            some = jnp.concatenate([keys(b) for b in blocks[4 * h : 4 * h + 4]], 0)
            scores.append(
                lax.dot_general(
                    q, some, (((1,), (1,)), ((), ())), preferred_element_type=jnp.float32
                )
            )
        return jnp.concatenate(scores, 1) * softmax_scale

    def soften(score, live):
        alive = lax.broadcasted_iota(jnp.int32, score.shape, 1) < live
        masked = jnp.where(alive, score, masked_score)
        highest = jnp.max(masked, 1, keepdims=True)
        weights = jnp.where(alive, jnp.exp(masked - highest), 0.0)
        summed = jnp.sum(weights, 1, keepdims=True)
        return weights.astype(jnp.bfloat16), 1.0 / summed, highest + jnp.log(summed)

    def value_of(weights_b, blocks):
        result = None
        for h in range(2):
            vals = jnp.concatenate([latents(b) for b in blocks[4 * h : 4 * h + 4]], 0)
            part = jnp.dot(
                weights_b[:, 256 * h : 256 * h + 256], vals, preferred_element_type=jnp.float32
            )
            result = part if result is None else result + part
        return result

    for o in range(owners):
        begin, end = ends[o], ends[o + 1]
        for copy in copies[o]:
            copy.wait()
        for copy in (copies[o + 1] if o + 1 < owners else []) + (extra if o == 0 else []):
            copy.start()

        def several(j, carry):
            first = begin + AT_ONCE * j
            group = [jnp.minimum(first + i, end - 1) for i in range(AT_ONCE)]
            for i, slot in enumerate(group):

                @pl.when(first + i < end)
                def _():
                    fetch(slot).wait()

            blocks = [blocks_of(slot) for slot in group]
            scores = [score_of(slot, some) for slot, some in zip(group, blocks)]
            soft = [soften(score, live_ref[items[slot]]) for score, slot in zip(scores, group)]
            results = [value_of(one[0], some) for one, some in zip(soft, blocks)]
            for slot, one, result in zip(group, soft, results):
                normal[slot] = result * one[1]
                slot_lse[slot] = jnp.broadcast_to(one[2], slot_lse.shape[1:])
            return carry

        lax.fori_loop(0, (end - begin + AT_ONCE - 1) // AT_ONCE, several, 0)

    for copy in extra:
        copy.wait()

    def project(group, carry):
        some = pl.ds(pl.multiple_of(group * 32, 32), 32)
        for j in range(8):
            span = slice(8 * j, 8 * j + 8)
            x = normal[some, span, :].reshape(32 * 8, LAT).astype(jnp.bfloat16)
            w = jnp.concatenate([w_ref[2 * j], w_ref[2 * j + 1]], 1)
            y = jnp.dot(x, w, preferred_element_type=jnp.float32)
            upper = (lax.broadcasted_iota(jnp.int32, (32 * 8, 128), 0) & 7) < 4
            projected[some, span, :] = jnp.where(upper, y[:, :128], y[:, 128:]).reshape(32, 8, 128)
        return carry

    lax.fori_loop(0, (found + 31) // 32, project, 0)
    if stage == "last":
        each(lambda slot: load_row(slot).start())
        each(lambda slot: load_row(slot).wait())

    diagonal = lax.broadcasted_iota(jnp.int32, (64, 128), 0) == lax.broadcasted_iota(
        jnp.int32, (64, 128), 1
    )
    for o in range(owners):
        begin, end = ends[o], ends[o + 1]

        def merge(j, carry):
            group = [jnp.minimum(begin + AT_ONCE * j + i, end - 1) for i in range(AT_ONCE)]
            where = [row_of(slot) for slot in group]
            values = []
            for slot, row in zip(group, where):
                across = jnp.broadcast_to(lse_ref[pl.ds(row, 1), :], (64, 128))
                before = jnp.sum(jnp.where(diagonal, across, 0.0), 1, keepdims=True)
                added = slot_lse[slot]
                most = jnp.maximum(before, added)
                keep = jnp.exp(before - most)
                add = jnp.exp(added - most)
                both = keep + add
                lse = most + jnp.log(both)
                lse_row = jnp.sum(jnp.where(diagonal, lse, 0.0), 0, keepdims=True)
                old = normal[slot, :, :128] if stage == "last" else state[row]
                values.append((lse_row, (old * keep + projected[slot] * add) / both))
            for slot, row, (lse_row, value) in zip(group, where, values):
                lse_ref[pl.ds(row, 1), :] = lse_row
                if stage == "last":
                    projected[slot] = value
                else:
                    state[row] = value
            return carry

        lax.fori_loop(0, (end - begin + AT_ONCE - 1) // AT_ONCE, merge, 0)
    if stage == "last":
        each(lambda slot: store_row(slot).start())
        each(lambda slot: store_row(slot).wait())


def attend(queries, w_uv, blocks, live, parity, arrays, pieces, base, owners, stage, after, earlier):
    rows = queries.shape[0]
    slots = owners * GROUP * 2
    all_blocks = (owners * 64,) if stage == "first" else (owners * 4 * PAIRS,)
    whole = pl.BlockSpec(memory_space=pltpu.VMEM)
    anywhere = pl.BlockSpec(memory_space=pltpu.HBM)
    in_specs = [anywhere, anywhere] + [anywhere] * len(arrays)
    in_specs += [anywhere] * len(after)
    operands = [queries, w_uv, *arrays, *after, *earlier]
    if earlier:
        in_specs += [anywhere, anywhere]
    return pl.pallas_call(
        functools.partial(attend_kernel, base, owners, pieces, len(after), stage),
        out_shape=[
            jax.ShapeDtypeStruct((rows, 64, 128), jnp.float32),
            jax.ShapeDtypeStruct((rows, 128), jnp.float32),
        ],
        grid_spec=pltpu.PrefetchScalarGridSpec(
            num_scalar_prefetch=3,
            grid=(),
            in_specs=in_specs,
            out_specs=[anywhere if stage == "last" else whole, whole],
            scratch_shapes=[
                pltpu.VMEM(all_blocks + arrays[0].shape[1:], jnp.bfloat16),
                pltpu.VMEM((slots, 64, WIDE), jnp.bfloat16),
                pltpu.VMEM((slots, 64, LAT), jnp.float32),
                pltpu.VMEM((slots, 64, 128), jnp.float32),
                pltpu.VMEM((slots, 64, 128), jnp.float32),
                pltpu.VMEM(w_uv.shape, w_uv.dtype),
                pltpu.SMEM((owners * rows,), jnp.int32),
                pltpu.SemaphoreType.DMA((len(arrays) + 3,)),
                pltpu.SemaphoreType.DMA((slots,)),
                pltpu.SemaphoreType.DMA((slots,)),
            ],
        ),
        input_output_aliases={3 + len(operands) - 2: 0} if stage == "last" else {},
        compiler_params=pltpu.CompilerParams(vmem_limit_bytes=VMEM_BYTES),
        cost_estimate=pl.CostEstimate(
            flops=owners * 32 * 64 * 512 * 1088 * 2,
            bytes_accessed=owners * 5 * 2**20 + 2**24,
            transcendentals=owners * 32 * 64 * 512,
        ),
    )(blocks, live, parity, *operands)


def tables(info, targets):
    slots = info[:, 0, :]
    owners = info[:, 1, :SEGS]
    lengths = info[:, 1, SEGS] * 64 + info[:, 1, SEGS + 1]
    rows = info.shape[0]
    segment = jnp.arange(SEGS, dtype=jnp.int32)
    match = (owners[None] == targets[:, None, None]).astype(jnp.int32)
    tokens = jnp.clip(lengths[:, None] - segment[None, :] * 512, 0, 512)
    live = jnp.sum(match * tokens[None], -1)
    blocks = jnp.sum(match[..., None] * slots.reshape(rows, SEGS, SEGS)[None], 2)
    return blocks.reshape(-1), live.reshape(-1)


def body(
    hidden, w_dkv, kv_gain, q_latent, q_rope, w_uv, latent_cache, block_slots, seg_owner, lengths
):
    row_count, step_count = hidden.shape[:2]
    channels = latent_cache.shape[-1]
    heads_dev = q_latent.shape[2] // LAT
    rope_width = channels - LAT
    me = lax.axis_index("cache")
    core = me % NC
    y_here = me // GROUP
    parity = lax.axis_index("tensor") % 2
    parities = parity.astype(jnp.int32)[None]
    half_a, half_b, lengths = pack(latent_cache, parities, lengths)
    positions = lengths[:, None] + jnp.arange(step_count, dtype=jnp.int32)[None, :]

    cosine, sine_part = angle_tables(positions, rope_width)

    roped = rotate(
        q_rope.reshape(row_count, step_count, heads_dev, rope_width).astype(jnp.float32),
        cosine[:, :, None],
        sine_part[:, :, None],
    ).astype(jnp.bfloat16)
    queries = jnp.concatenate(
        [q_latent.reshape(row_count, step_count, heads_dev, LAT), roped], -1
    ).swapaxes(1, 2)
    queries = queries.reshape(row_count, heads_dev * step_count, channels)
    second = jnp.concatenate([seg_owner, lengths[:, None] // 64, lengths[:, None] % 64], 1)
    second = jnp.pad(second, ((0, 0), (0, 64 - second.shape[1])))
    info = jnp.stack([block_slots, second], 1).astype(jnp.bfloat16)
    info = jnp.pad(info, ((0, 0), (0, heads_dev * step_count - 2), (0, 0)))
    message = jnp.concatenate([queries, info], -1)
    all_queries = lax.all_gather(
        message,
        "cache",
        axis=0,
        tiled=True,
        axis_index_groups=[[y * GROUP + i for i in range(GROUP)] for y in range(NY)],
    )

    nothing = jnp.minimum(lengths[0], 0).astype(hidden.dtype)
    partial_sum = jnp.einsum("rsd,dc->rsc", hidden + nothing, w_dkv, preferred_element_type=jnp.float32)
    summed = lax.psum(partial_sum, "tensor")
    m_a = along_y(half_a, 1)
    p_b = along_y(half_b, -1)
    half_a, half_b, m_a, p_b = gate(half_a, half_b, m_a, p_b)
    m_b = along_y(half_b, 1)
    p_a = along_y(half_a, -1)
    m_l = along_x(m_a, 1)
    p_r = along_x(p_b, -1)
    m_b, p_a, m_l, p_r, m_a, p_b, summed = gate(m_b, p_a, m_l, p_r, m_a, p_b, summed)
    t_a = along_y(m_a, 1)
    t_b = along_y(p_b, -1)
    m_r = along_x(m_b, -1)
    p_l = along_x(p_a, 1)
    new_latent = finish_latent(summed, cosine, sine_part, kv_gain)
    own_scores = (
        jnp.einsum("rqc,rtc->rqt", queries, new_latent, preferred_element_type=jnp.float32)
        * softmax_scale
    )
    steps_of = jnp.arange(heads_dev * step_count) % step_count
    causal = (jnp.arange(step_count)[None, :] <= steps_of[:, None])[None]
    own_masked = jnp.where(causal, own_scores, masked_score)
    own_top = jnp.max(own_masked, -1)
    own_weights = jnp.where(causal, jnp.exp(own_masked - own_top[..., None]), 0.0)
    own_total = jnp.sum(own_weights, -1)
    own_sum = jnp.einsum("rqt,rtl->rql", own_weights, new_latent[..., :LAT].astype(jnp.float32))
    own_b = own_sum.astype(jnp.bfloat16).reshape(row_count, heads_dev, step_count, LAT)
    own_proj = jnp.einsum("rhsl,hlv->rhsv", own_b, w_uv, preferred_element_type=jnp.float32)
    own_proj = own_proj.reshape(row_count, heads_dev * step_count, -1)
    own_part = own_proj / own_total[..., None]
    own_lse = own_top + jnp.log(own_total)

    table = all_queries[:, :2, channels:].astype(jnp.float32).astype(jnp.int32)
    offsets = jnp.array([0, NY - 1, 1, 2], jnp.int32)
    targets = (y_here + offsets) % NY * GROUP + me % GROUP

    blocks, live = tables(table, targets)

    def stage_of(name, base, lists, after, earlier=()):
        pieces, arrays = [], []
        for owner, quarters in enumerate(lists):
            if quarters is None:
                pieces.append((owner, "all", 0))
                arrays.append(latent_cache)
            else:
                for which, quarter in enumerate(quarters):
                    offset = which % 2 * PAIRS
                    for array in quarter if isinstance(quarter, tuple) else (quarter,):
                        pieces.append((owner, "mine" if which < 2 else "other", offset))
                        arrays.append(array)
                        offset += array.shape[0]
        return attend(
            all_queries,
            w_uv,
            blocks,
            live,
            parities,
            arrays,
            pieces,
            base,
            len(lists),
            name,
            after,
            earlier,
        )

    state = stage_of("first", 0, [None], (m_l, p_r))
    part_l, part_r = m_l[PAIRS // 2 :], p_r[PAIRS // 2 :]
    t_a, t_b, m_r, p_l, part_l, part_r, own_lse, *state = gate(
        t_a, t_b, m_r, p_l, part_l, part_r, own_lse, *state
    )
    t_l = (along_x(t_a[: PAIRS // 2], 1), along_y(part_l, 1))
    t_r = (along_x(t_b[: PAIRS // 2], -1), along_y(part_r, -1))
    state = stage_of(
        "middle",
        1,
        [(m_a, m_b, m_l, m_r), (p_a, p_b, p_l, p_r)],
        (t_a, t_b),
        tuple(state),
    )
    part, lse = stage_of("last", 3, [(t_a, t_b, t_l, t_r)], (), tuple(state))

    width = part.shape[1]
    part = part.reshape(NZ, NC, row_count, width, -1)
    lse = lse[:, :width].reshape(NZ, NC, row_count, width)
    pick = lambda array, which: lax.dynamic_index_in_dim(array, which, 1, keepdims=False)
    theirs = other_core(pick(part, 1 - core).astype(jnp.bfloat16))
    part, theirs = gate(part, theirs)
    mine = pick(part, core)
    lse_mine, lse_theirs = pick(lse, core), other_core(pick(lse, 1 - core))
    most = jnp.maximum(lse_mine, lse_theirs)
    w_mine, w_theirs = jnp.exp(lse_mine - most), jnp.exp(lse_theirs - most)
    both = w_mine + w_theirs
    chip_part = mine * (w_mine / both)[..., None] + theirs * (w_theirs / both)[..., None]
    chip_lse = most + jnp.log(both)
    nearest = lambda array: lax.reduce_precision(array, 8, 7)
    high = nearest(chip_lse)
    middle = nearest(chip_lse - high)
    low = chip_lse - high - middle
    stats = jnp.concatenate(
        [jnp.concatenate([high, middle], 2), jnp.concatenate([low, jnp.zeros_like(low)], 2)], 1
    ).astype(jnp.bfloat16)
    chip_part = chip_part.astype(jnp.bfloat16).reshape(NZ, row_count * width, -1)
    along_z = [[place(y, z, c) for z in range(NZ)] for y in range(NY) for c in range(NC)]
    got = lax.all_to_all(
        jnp.concatenate([chip_part, stats], 1),
        "cache",
        split_axis=0,
        concat_axis=0,
        axis_index_groups=along_z,
        tiled=True,
    )
    home_part = got[:, : row_count * width].reshape(NZ, row_count, width, -1)
    stats = got[:, row_count * width :].astype(jnp.float32)
    home_lse = (
        stats[:, :row_count, :width] + stats[:, :row_count, width:]
    ) + stats[:, row_count:, :width]
    largest = jnp.maximum(own_lse, jnp.max(home_lse, 0))
    factor = jnp.exp(home_lse - largest[None])
    own_factor = jnp.exp(own_lse - largest)
    numerator = jnp.sum(factor[..., None] * home_part, 0) + own_factor[..., None] * own_part
    denominator = jnp.sum(factor, 0) + own_factor
    attn_out = (numerator / denominator[..., None]).astype(jnp.bfloat16)
    attn_out = attn_out.reshape(row_count, heads_dev, step_count, -1).swapaxes(1, 2)
    return (attn_out.reshape(row_count, step_count, -1), new_latent)


def solution(mesh):
    in_specs = (
        P("cache", None, "tensor"),
        P("tensor", None),
        P(),
        P("cache", None, "tensor"),
        P("cache", None, "tensor"),
        P("tensor", None, None),
        P("cache", None, None),
        P("cache", None),
        P("cache", None),
        P("cache"),
    )
    out_specs = (P("cache", None, "tensor"), P("cache", None, None))
    return jax.shard_map(body, mesh=mesh, in_specs=in_specs, out_specs=out_specs, check_vma=False)
```
